32 devices in a mesh: tr: 4 (over x, core), gz: 8 (over z, y).
Axes of the slice: x: 2, y: 2, z: 4, core: 2. Of those that a mesh axis runs over, the one named last changes fastest.
Arguments:
- tokens: bfloat16 [40, 32, 8, 768], P('gz', None, 'tr'), may hold values from -6 to 6
- cotangent: bfloat16 [40, 32, 8, 768], P('gz', None, 'tr'), may hold values from -6 to 6
- gain_x: float32 [768], replicated, may hold values from 0.1 to 1.9
- wqkv_x: bfloat16 [768, 2304], P('tr'), as said below
- wo_x: bfloat16 [768, 768], P('tr'), may hold values from -0.21875 to 0.21875
- gain_z: float32 [768], replicated, may hold values from 0.1 to 1.9
- wqkv_z: bfloat16 [768, 2304], P('tr'), as said below
- wo_z: bfloat16 [768, 768], P('tr'), may hold values from -0.21875 to 0.21875
Outputs:
- grad_tokens: bfloat16 [40, 32, 8, 768], P('gz', None, 'tr')
The draws below stay inside these ranges and needn't reach their ends.
Inputs may be any that keep to these rules, and one draw needn't show every extreme that they name: `wqkv_x`: query, key and value columns side by side, each block split into 6 heads of 128. `wqkv_z`: query, key and value columns side by side, each block split into 6 heads of 128.
All inputs are finite; a program needn't handle non-finite values.
Results may differ from the reference program's by a relative error of at most 0.038.
The reference program's roundings to bfloat16 on the way count: a program that leaves them out, or rounds other values in their place, can miss the bound.
Values may be sent and summed in bfloat16 or wider, within the bound.
A program may use at most 64 MiB of HBM per device.

```python
import jax
import jax.numpy as jnp
from jax import lax

H = 6
HD = 128
D = 768
Y = 32
X = 8
Z = 40


def projection_draw(key):
    base = jnp.clip(jax.random.normal(key, (D, 3 * D), jnp.float32), -6.0, 6.0) * D ** (-0.5)
    return base


def draw_wqkv_x(key, part):
    return projection_draw(jax.random.fold_in(key, 3)).astype(jnp.bfloat16)


def draw_wqkv_z(key, part):
    return projection_draw(jax.random.fold_in(key, 5)).astype(jnp.bfloat16)


def level_of(rng, extent, split, least, top_value):
    factor_of, own = 1.0, jax.random.fold_in(rng, 6)
    for dim, shards_of in split:
        heights = jnp.exp(jax.random.uniform(jax.random.fold_in(own, dim), (shards_of,), jnp.float32, least / len(split), top_value / len(split)))
        factor_of = factor_of * jnp.repeat(heights, extent[dim] // shards_of).reshape([-1 if axis == dim else 1 for axis in range(len(extent))])
    return factor_of


def gaussian(stream_key, dims, width, bound, shards=(), kind=jnp.bfloat16):
    result = jax.random.normal(stream_key, dims, jnp.float32) * width
    if len(shards) > 0:
        result = level_of(stream_key, dims, shards, -0.22, 0.18) * result
    return jnp.clip(result, min=-bound, max=bound).astype(kind)


def setup_inputs(seed: int = 0) -> dict:
    keys = jax.random.split(jax.random.key(seed), 9)
    return {
        "tokens": gaussian(keys[0], (Z, Y, X, D), 1.0, 6.0, ((0, 8), (2, 4))),
        "cotangent": gaussian(keys[1], (Z, Y, X, D), 1.0, 6.0, ((0, 8), (2, 4))),
        "gain_x": jnp.clip(1.0 + 0.18 * jax.random.normal(keys[2], (D,), jnp.float32), 0.1, 1.9),
        "wqkv_x": draw_wqkv_x(jax.random.fold_in(keys[8], 71), 0),
        "wo_x": gaussian(keys[4], (D, D), D ** -0.5, 0.21875, ((0, 4),)),
        "gain_z": jnp.clip(1.0 + 0.18 * jax.random.normal(keys[5], (D,), jnp.float32), 0.1, 1.9),
        "wqkv_z": draw_wqkv_z(jax.random.fold_in(keys[8], 71), 0),
        "wo_z": gaussian(keys[7], (D, D), D ** -0.5, 0.21875, ((0, 4),)),
    }


def rounded(value):
    return lax.optimization_barrier(value.astype(jnp.bfloat16))

def head_split(packed, index):
    width_all = packed.shape[-1] // 3
    piece = packed[..., index * width_all:(index + 1) * width_all]
    return piece.reshape(piece.shape[:-1] + (H, HD))

def merge_heads(value):
    return value.reshape(value.shape[:-2] + (H * HD,))

def recompute(tokens_in, gain_vec, w_in, layout):
    widened = tokens_in.astype(jnp.float32)
    inv_rms = lax.rsqrt(lax.optimization_barrier(jnp.mean(widened * widened, axis=-1, keepdims=True)) + 1e-06)
    normed = rounded(widened * inv_rms * gain_vec)
    packed = rounded(jnp.dot(normed, w_in, preferred_element_type=jnp.float32))
    queries = head_split(packed, 0).astype(jnp.float32)
    key_part = head_split(packed, 1).astype(jnp.float32)
    values = head_split(packed, 2).astype(jnp.float32)
    key_form = layout.replace('l', 'm')
    scores = jnp.einsum(layout + ',' + key_form + '->bhlm', queries, key_part) * HD ** (-0.5)
    probs = jax.nn.softmax(scores, axis=-1)
    probs_b = rounded(probs).astype(jnp.float32)
    return (widened, inv_rms, queries, key_part, values, probs, probs_b)

def forward_out(tokens_in, gain_vec, w_in, w_out, layout):
    widened, inv_rms, queries, key_part, values, probs, probs_b = recompute(tokens_in, gain_vec, w_in, layout)
    key_form = layout.replace('l', 'm')
    mixed = rounded(merge_heads(jnp.einsum('bhlm,' + key_form + '->' + layout, probs_b, values)))
    return (widened + jnp.dot(mixed, w_out, preferred_element_type=jnp.float32)).astype(jnp.bfloat16)

def backward(tokens_in, upstream, gain_vec, w_in, w_out, layout):
    widened, inv_rms, queries, key_part, values, probs, probs_b = recompute(tokens_in, gain_vec, w_in, layout)
    key_form = layout.replace('l', 'm')
    d_mixed = rounded(jnp.dot(upstream, w_out.T, preferred_element_type=jnp.float32))
    d_mixed = d_mixed.reshape(d_mixed.shape[:-1] + (H, HD)).astype(jnp.float32)
    d_probs = jnp.einsum(layout + ',' + key_form + '->bhlm', d_mixed, values)
    d_values = rounded(jnp.einsum('bhlm,' + layout + '->' + key_form, probs_b, d_mixed))
    centre = lax.optimization_barrier(jnp.sum(probs * d_probs, axis=-1, keepdims=True))
    d_scores = rounded(probs * (d_probs - centre) * HD ** (-0.5)).astype(jnp.float32)
    d_queries = rounded(jnp.einsum('bhlm,' + key_form + '->' + layout, d_scores, key_part))
    d_keys = rounded(jnp.einsum('bhlm,' + layout + '->' + key_form, d_scores, queries))
    joined = jnp.concatenate([merge_heads(d_queries), merge_heads(d_keys), merge_heads(d_values)], axis=-1)
    d_normed = jnp.dot(joined, w_in.T, preferred_element_type=jnp.float32)
    scaled = d_normed * gain_vec
    d_tokens = inv_rms * (scaled - widened * inv_rms * inv_rms * lax.optimization_barrier(jnp.mean(scaled * widened, axis=-1, keepdims=True)))
    return (upstream.astype(jnp.float32) + d_tokens).astype(jnp.bfloat16)

def reference(tokens, cotangent, gain_x, wqkv_x, wo_x, gain_z, wqkv_z, wo_z):
    mid = lax.map(lambda plane: forward_out(plane, gain_x, wqkv_x, wo_x, 'blhe'), tokens)
    columns = jnp.transpose(mid, (1, 0, 2, 3))
    cot_columns = jnp.transpose(cotangent, (1, 0, 2, 3))
    grad_columns = lax.map(lambda pair: backward(pair[0], pair[1], gain_z, wqkv_z, wo_z, 'lbhe'), (columns, cot_columns))
    grad_mid = jnp.transpose(grad_columns, (1, 0, 2, 3))
    return lax.map(lambda pair: backward(pair[0], pair[1], gain_x, wqkv_x, wo_x, 'blhe'), (tokens, grad_mid))
```

```python
import functools
import math

import jax
import jax.numpy as jnp
import numpy as np
from jax import lax
from jax.experimental import pallas as pl
from jax.experimental.pallas import tpu as pltpu
from jax.sharding import PartitionSpec as P

H = 6


def head_split(packed, index, model_width):
    piece = packed[..., index * model_width : (index + 1) * model_width]
    return piece.reshape(piece.shape[:-1] + (H, model_width // H))


def merge_heads(value):
    return value.reshape(value.shape[:-2] + (value.shape[-2] * value.shape[-1],))


def recompute(tokens_in, gain_vec, w_in, layout):
    model_width = w_in.shape[0]
    factor = 1.0 / math.sqrt(model_width // H)
    widened = tokens_in.astype(jnp.float32)
    inv_rms = lax.rsqrt(jnp.mean(widened * widened, axis=-1, keepdims=True) + 1e-06)
    normed = (widened * inv_rms * gain_vec).astype(jnp.bfloat16)
    packed = jnp.dot(normed, w_in, preferred_element_type=jnp.float32).astype(jnp.bfloat16)
    queries = head_split(packed, 0, model_width)
    key_part = head_split(packed, 1, model_width)
    values = head_split(packed, 2, model_width)
    key_form = layout.replace("l", "m")
    scores = (
        jnp.einsum(
            layout + "," + key_form + "->bhlm",
            queries,
            key_part,
            preferred_element_type=jnp.float32,
        )
        * factor
    )
    highest = jnp.max(scores, axis=-1, keepdims=True)
    expanded = jnp.exp(scores - highest)
    probs = expanded / jnp.sum(expanded, axis=-1, keepdims=True)
    return (widened, inv_rms, queries, key_part, values, probs, probs.astype(jnp.bfloat16), factor)


def forward_out(tokens_in, gain_vec, w_in, w_out, layout):
    widened, inv_rms, queries, key_part, values, probs, probs_b, factor = recompute(
        tokens_in, gain_vec, w_in, layout
    )
    key_form = layout.replace("l", "m")
    mixed = jnp.einsum(
        "bhlm," + key_form + "->" + layout, probs_b, values, preferred_element_type=jnp.float32
    )
    mixed = merge_heads(mixed.astype(jnp.bfloat16))
    return (widened + jnp.dot(mixed, w_out, preferred_element_type=jnp.float32)).astype(
        jnp.bfloat16
    )


def backward(tokens_in, upstream, gain_vec, w_in, w_out, layout):
    widened, inv_rms, queries, key_part, values, probs, probs_b, factor = recompute(
        tokens_in, gain_vec, w_in, layout
    )
    key_form = layout.replace("l", "m")
    d_mixed = jnp.dot(upstream, w_out.T, preferred_element_type=jnp.float32).astype(jnp.bfloat16)
    d_mixed = d_mixed.reshape(d_mixed.shape[:-1] + (H, d_mixed.shape[-1] // H))
    d_probs = jnp.einsum(
        layout + "," + key_form + "->bhlm", d_mixed, values, preferred_element_type=jnp.float32
    )
    d_values = jnp.einsum(
        "bhlm," + layout + "->" + key_form, probs_b, d_mixed, preferred_element_type=jnp.float32
    ).astype(jnp.bfloat16)
    centre = jnp.sum(probs * d_probs, axis=-1, keepdims=True)
    d_scores = (probs * (d_probs - centre) * factor).astype(jnp.bfloat16)
    d_queries = jnp.einsum(
        "bhlm," + key_form + "->" + layout, d_scores, key_part, preferred_element_type=jnp.float32
    ).astype(jnp.bfloat16)
    d_keys = jnp.einsum(
        "bhlm," + layout + "->" + key_form, d_scores, queries, preferred_element_type=jnp.float32
    ).astype(jnp.bfloat16)
    joined = jnp.concatenate(
        [merge_heads(d_queries), merge_heads(d_keys), merge_heads(d_values)], axis=-1
    )
    d_normed = jnp.dot(joined, w_in.T, preferred_element_type=jnp.float32)
    scaled = d_normed * gain_vec
    d_tokens = inv_rms * (
        scaled - widened * inv_rms * inv_rms * jnp.mean(scaled * widened, axis=-1, keepdims=True)
    )
    return (upstream.astype(jnp.float32) + d_tokens).astype(jnp.bfloat16)


def line_forward(lines, gain_vec, w_in, w_out):
    feature_count = lines.shape[3]
    flat = lines.reshape(-1, lines.shape[2], feature_count)
    return forward_out(flat, gain_vec, w_in, w_out, "blhe").reshape(lines.shape)


def line_backward(lines, upstream, gain_vec, w_in, w_out):
    feature_count = lines.shape[3]
    flat = lines.reshape(-1, lines.shape[2], feature_count)
    flat_up = upstream.reshape(flat.shape)
    return backward(flat, flat_up, gain_vec, w_in, w_out, "blhe").reshape(lines.shape)


def per_device(tokens, cotangent, gain_x, wqkv_x, wo_x, gain_z, wqkv_z, wo_z):
    full_in_x, full_out_x = (
        lax.all_gather(wqkv_x, "tr", axis=0, tiled=True),
        lax.all_gather(wo_x, "tr", axis=0, tiled=True),
    )
    full_in_z, full_out_z = (
        lax.all_gather(wqkv_z, "tr", axis=0, tiled=True),
        lax.all_gather(wo_z, "tr", axis=0, tiled=True),
    )
    width = tokens.shape[-1]
    lines = lax.all_to_all(tokens, "tr", split_axis=1, concat_axis=2, tiled=True)
    cot_lines = lax.all_to_all(cotangent, "tr", split_axis=1, concat_axis=2, tiled=True)
    cells = lines.shape[1] * lines.shape[2]
    flat = (lines.shape[0], cells, width)
    cot_columns = lax.all_to_all(
        cot_lines.reshape(flat), "gz", split_axis=1, concat_axis=0, tiled=True
    )
    mid_lines = line_forward(lines, gain_x, full_in_x, full_out_x)
    mid_columns = lax.all_to_all(
        mid_lines.reshape(flat), "gz", split_axis=1, concat_axis=0, tiled=True
    )
    grad_columns = backward(
        mid_columns, cot_columns, gain_z, full_in_z, full_out_z, "lbhe"
    )
    grad_lines = lax.all_to_all(grad_columns, "gz", split_axis=0, concat_axis=1, tiled=True)
    result_lines = line_backward(lines, grad_lines.reshape(lines.shape), gain_x, full_in_x, full_out_x)
    return lax.all_to_all(result_lines, "tr", split_axis=2, concat_axis=1, tiled=True)


F32, BF16 = jnp.float32, jnp.bfloat16


def nt(a, b):
    return lax.dot_general(a, b, (((1,), (1,)), ((), ())), preferred_element_type=F32)


def tn(a, b):
    return lax.dot_general(a, b, (((0,), (0,)), ((), ())), preferred_element_type=F32)


def nn(a, b):
    return jnp.dot(a, b, preferred_element_type=F32)


def rms(a):
    return lax.rsqrt(jnp.mean(a * a, axis=-1, keepdims=True) + 1e-06)


def project(a, rstd, gain, w, qkv):
    width = a.shape[1]
    normed = (a * rstd * gain).astype(BF16)
    for j in range(3):
        cols = slice(j * width, (j + 1) * width)
        qkv[:, cols] = nn(normed, w[:, cols]).astype(BF16)


def line_mask(block, line, inner):
    key = lax.broadcasted_iota(jnp.int32, (block, block), 0)
    query = lax.broadcasted_iota(jnp.int32, (block, block), 1)
    if inner:
        return key % line == query % line
    return key // line == query // line


def head_spans(width):
    size = width // H
    return [[pl.ds(n * width + h * size, size) for n in range(3)] for h in range(H)]


def softmax_rows(qkv, at, spans, mask, factor):
    qk = [nt(qkv[at, sp[1]], qkv[at, sp[0]]) for sp in spans]
    scores = [jnp.where(mask, x * factor, -1e30) for x in qk]
    tops = [jnp.max(x, axis=0, keepdims=True) for x in scores]
    grown = [jnp.exp(x - t) for x, t in zip(scores, tops)]
    sums = [1.0 / jnp.sum(x, axis=0, keepdims=True) for x in grown]
    return [x * t for x, t in zip(grown, sums)]


def attend_forward(qkv, probs, first, mixed, mask):
    rows, width = mixed.shape
    block = mask.shape[0]
    factor = 1.0 / math.sqrt(width // H)
    spans = head_spans(width)
    for b in range(rows // block):
        at = pl.ds(b * block, block)
        ps = softmax_rows(qkv, at, spans, mask, factor)
        for h, p in enumerate(ps):
            probs[(first + b) * H + h] = p
        outs = [tn(p.astype(BF16), qkv[at, sp[2]]) for p, sp in zip(ps, spans)]
        for sp, o in zip(spans, outs):
            mixed[at, sp[0]] = o.astype(BF16)


def attend_backward(qkv, probs, first, d_mixed, joined, mask, keep):
    rows, width = d_mixed.shape
    block = mask.shape[0]
    factor = 1.0 / math.sqrt(width // H)
    spans = head_spans(width)
    for b in range(rows // block):
        at = pl.ds(b * block, block)
        dps = [nt(qkv[at, sp[2]], d_mixed[at, sp[0]]) for sp in spans]
        if keep:
            ps = [probs[(first + b) * H + h] for h in range(H)]
        else:
            ps = softmax_rows(qkv, at, spans, mask, factor)
        dvs = [nn(p.astype(BF16), d_mixed[at, sp[0]]) for p, sp in zip(ps, spans)]
        centres = [jnp.sum(p * dp, axis=0, keepdims=True) for p, dp in zip(ps, dps)]
        dss = [(p * (dp - c) * factor).astype(BF16) for p, dp, c in zip(ps, dps, centres)]
        dks = [nn(ds, qkv[at, sp[0]]) for ds, sp in zip(dss, spans)]
        dqs = [tn(ds, qkv[at, sp[1]]) for ds, sp in zip(dss, spans)]
        for sp, dq, dk, dv in zip(spans, dqs, dks, dvs):
            joined[at, sp[0]] = dq.astype(BF16)
            joined[at, sp[1]] = dk.astype(BF16)
            joined[at, sp[2]] = dv.astype(BF16)


def norm_backward(a, c, rstd, gain, joined, w, dn):
    width = a.shape[-1]
    part = width // 3
    for j in range(3):
        dn[:, j * part : (j + 1) * part] = nt(joined[...], w[j * part : (j + 1) * part, :])
    scaled = dn[...] * gain
    mean = jnp.mean(scaled * a, axis=-1, keepdims=True)
    return (c + rstd * (scaled - a * (rstd * rstd) * mean)).astype(BF16)


def kernel(
    nt_, ng, line_x,
    tok, cot, gain_x, wx, ox, gain_z, wz, oz, out,
    tokr, cotr, cotz, mids, midr, grads, gradr, outs,
    fwx, fox, fwz, foz, qkvx, qkvz, probs, mixed, dmix, joined, dn, ax, az, cz,
    tr_send, tr_recv, gz_send, gz_recv, w_send, w_recv, local,
):
    me, mine = lax.axis_index("tr"), lax.axis_index("gz")
    sib, across = me + 1 - 2 * (me % 2), (me + 2) % nt_
    gy, gp = mine % 2, (mine // 2) % 2
    ynbr, znbr = mine + 1 - 2 * gy, mine + 2 - 4 * gp
    slab, pairs, width = tok.shape[0], tok.shape[3], tok.shape[5]
    parts = tok.shape[2]
    half = ax.shape[0] // parts
    block = half // 2

    barrier = pltpu.get_barrier_semaphore()
    for d in range(1, nt_):
        pl.semaphore_signal(barrier, inc=1, device_id=((me + d) % nt_, mine), device_id_type=pl.DeviceIdType.MESH)
    for d in range(1, ng):
        pl.semaphore_signal(barrier, inc=1, device_id=(me, (mine + d) % ng), device_id_type=pl.DeviceIdType.MESH)

    own_w = ((wx, wx, wx, ox), (wz, wz, wz, oz))
    full_w = ((fwx, fwx, fwx, fox), (fwz, fwz, fwz, foz))
    depth = wx.shape[0]
    quarter = depth // 4

    here = [
        pltpu.make_async_copy(tok.at[:, me], tokr.at[:, :, :, me], local.at[0]),
        pltpu.make_async_copy(cot.at[:, me], cotr.at[:, :, :, me // 2, me % 2], local.at[1]),
    ]
    for s in range(2):
        for k in (0, 3):
            to = full_w[s][k].at[pl.ds(pl.multiple_of(me * depth, 16), depth)]
            here.append(pltpu.make_async_copy(own_w[s][k], to, local.at[len(here)]))
    for copy in here:
        copy.start()

    pl.semaphore_wait(barrier, nt_ + ng - 2)

    def remote(src, dst, send, recv, t, g):
        return pltpu.make_async_remote_copy(
            src_ref=src, dst_ref=dst, send_sem=send, recv_sem=recv,
            device_id=(t, g), device_id_type=pl.DeviceIdType.MESH,
        )

    def own(s, k, row, n):
        at = pl.ds(pl.multiple_of(row, 16), n)
        return own_w[s][k].at[at, pl.ds((k % 3) * width, width)]

    def spot(s, k, shard, row, n):
        at = pl.ds(pl.multiple_of(shard * depth + row, 16), n)
        return full_w[s][k].at[at, pl.ds((k % 3) * width, width)]

    def push(s, k, role, src, dst, t, g):
        return remote(src, dst, w_send.at[s, k, role], w_recv.at[s, k, role], t, g)

    q_me, q_y = (2 * gy + gp) * quarter, (2 - 2 * gy + gp) * quarter
    q_z, q_d = (2 * gy + 1 - gp) * quarter, (3 - 2 * gy - gp) * quarter
    by_z = (0, 1)

    def direct_rows(s, k):
        if s == 0:
            return q_me, quarter
        n = DIRECT[k] * quarter
        return gy * (depth - n), n

    def relay_rows(s, k, y):
        if s == 0:
            return (2 * (1 - y) + gp) * quarter, quarter
        n = DIRECT[k] * quarter
        return (1 - y) * n, depth - n

    def role0(s, k):
        row, n = direct_rows(s, k)
        return push(s, k, 0, own(s, k, row, n), spot(s, k, me, row, n), across, mine)

    def role1(s, k):
        return push(s, k, 1, own(s, k, 0, depth), spot(s, k, me, 0, depth), sib, mine)

    def role2(s, k):
        row, n = relay_rows(s, k, 1 - gy)
        at = spot(s, k, across, row, n)
        return push(s, k, 2, at, at, me, ynbr)

    def role3(k):
        at = spot(0, k, across, q_me, quarter)
        return push(0, k, 3, at, at, me, znbr)

    def role4(k):
        if k in by_z:
            at = spot(0, k, across, q_y, quarter)
            return push(0, k, 4, at, at, me, znbr)
        at = spot(0, k, across, q_z, quarter)
        return push(0, k, 4, at, at, me, ynbr)

    def role5(s, k):
        at = spot(s, k, across, 0, depth)
        return push(s, k, 5, at, at, sib, mine)

    def arrived(s, k, role):
        if role == 0:
            at = spot(s, k, across, *direct_rows(s, k))
        elif role == 1:
            at = spot(s, k, sib, 0, depth)
        elif role == 2:
            at = spot(s, k, across, *relay_rows(s, k, gy))
        elif role == 3:
            at = spot(0, k, across, q_z, quarter)
        elif role == 4:
            at = spot(0, k, across, q_d, quarter)
        else:
            at = spot(s, k, (sib + 2) % nt_, 0, depth)
        push(s, k, role, at, at, sib, mine).wait_recv()

    def tr_copy(n, d):
        t = (me + d) % nt_
        src, dst = tr_ends(n, t, me)
        return remote(src, dst, tr_send.at[n, d], tr_recv.at[n, d], t, mine)

    def tr_ends(n, to, source):
        if n == 0:
            return tok.at[:, to], tokr.at[:, :, :, source]
        if n == 1:
            return cot.at[:, to], cotr.at[:, :, :, source // 2, source % 2]
        return outs.at[n - 2, :, :, to], out.at[:, source, n - 2]

    def gz_ends(n, to, source):
        if n == 0:
            return cotr.at[:, :, to // 2, :, to % 2], cotz.at[pl.ds(source * slab, slab)]
        if n <= 2:
            h = n - 1
            return mids.at[h, :, to // 2, :, to % 2], midr.at[h, pl.ds(source * slab, slab)]
        h = n - 3
        return grads.at[h, pl.ds(to * slab, slab)], gradr.at[h, :, source // 2, :, source % 2]

    def gz_copy(n, d):
        g = (mine + d) % ng
        src, dst = gz_ends(n, g, mine)
        return remote(src, dst, gz_send.at[n, d], gz_recv.at[n, d], me, g)

    far_first = [2, 3, 1] if nt_ == 4 else list(range(1, nt_))
    gz_order = sorted(range(1, ng), key=lambda d: -min(d, ng - d))

    def tr_begin(n):
        for d in far_first:
            tr_copy(n, d).start()

    def tr_end(n):
        for d in range(1, nt_):
            tr_copy(n, d).wait_send()
            src = (me + nt_ - d) % nt_
            at = tr_ends(n, me, src)[1]
            remote(at, at, tr_send.at[n, d], tr_recv.at[n, d], src, mine).wait_recv()

    def gz_begin(n):
        for d in gz_order:
            gz_copy(n, d).start()

    def gz_end(n):
        for d in range(1, ng):
            gz_copy(n, d).wait_send()
            src = (mine + ng - d) % ng
            at = gz_ends(n, mine, src)[1]
            remote(at, at, gz_send.at[n, d], gz_recv.at[n, d], me, src).wait_recv()

    ks = range(4)

    for k in ks:
        role0(0, k).start()
    for k in ks:
        role1(0, k).start()
    for k in ks:
        arrived(0, k, 0)
        role2(0, k).start()
        role3(k).start()
        if k == TOK_AFTER:
            tr_begin(0)
    for k in ks:
        arrived(0, k, 2)
        if k in by_z:
            role4(k).start()
        arrived(0, k, 3)
        if k not in by_z:
            role4(k).start()
    for k in ks:
        arrived(0, k, 4)
        role5(0, k).start()
    for copy in here:
        copy.wait()
    tr_end(0)
    tr_begin(1)
    for k in ks:
        role0(1, k).start()
    for k in ks:
        role1(1, k).start()
    for h in range(parts):
        ax[pl.ds(h * half, half)] = tokr[:, h].reshape(half, width)
    for k in ks:
        arrived(0, k, 1)
        arrived(0, k, 5)

    def relay_z(pieces):
        for k in pieces:
            arrived(1, k, 0)
            role2(1, k).start()

    mask_x = line_mask(block, line_x, False)
    mask_z = line_mask(block, block // (slab * ng), True)
    gx, gz = gain_x[...][None], gain_z[...][None]
    rstd_x = []
    for h in range(parts):
        at = pl.ds(h * half, half)
        a = ax[at].astype(F32)
        rstd_x.append(rms(a))
        project(a, rstd_x[h], gx, fwx, qkvx.at[at])
        attend_forward(qkvx.at[at], probs, 2 * h, mixed.at[at], mask_x)
        mid = ax[at].astype(F32) + nn(mixed[at], fox[...])
        mids[h] = mid.astype(BF16).reshape(mids.shape[1:])
        gz_begin(1 + h)
        midr[h, pl.ds(mine * slab, slab)] = mids[h, :, mine // 2, :, mine % 2]
        if h == 0:
            tr_end(1)
            gz_begin(0)
            cotz[pl.ds(mine * slab, slab)] = cotr[:, :, mine // 2, :, mine % 2]
            relay_z((0,))
    relay_z((1, 2, 3))
    for k in ks:
        arrived(1, k, 2)
        role5(1, k).start()
    for k in ks:
        arrived(1, k, 1)
        arrived(1, k, 5)
    gz_end(0)

    for h in range(parts):
        at = pl.ds(h * half, half)
        for j in range(2):
            cz[pl.ds(h * half + j * block, block)] = cotz[:, h, j].reshape(block, width)
        dmix[at] = nt(cz[at], foz[...]).astype(BF16)
    for h in range(parts):
        at = pl.ds(h * half, half)
        gz_end(1 + h)
        for j in range(2):
            az[pl.ds(h * half + j * block, block)] = midr[h, :, j].reshape(block, width)
        a = az[at].astype(F32)
        rstd = rms(a)
        project(a, rstd, gz, fwz, qkvz.at[at])
        attend_backward(qkvz.at[at], probs, 0, dmix.at[at], joined.at[at], mask_z, False)
        back = norm_backward(
            az[at].astype(F32), cz[at].astype(F32), rstd, gz, joined.at[at], fwz, dn.at[at]
        )
        for j in range(2):
            grads[h, :, j] = back[j * block : (j + 1) * block].reshape(slab * ng, block // (slab * ng), width)
        gz_begin(3 + h)
        gradr[h, :, mine // 2, :, mine % 2] = grads[h, pl.ds(mine * slab, slab)]

    kept = []
    for h in range(parts):
        at = pl.ds(h * half, half)
        gz_end(3 + h)
        c = gradr[h].reshape(half, width)
        dmix[at] = nt(c, fox[...]).astype(BF16)
        attend_backward(qkvx.at[at], probs, 2 * h, dmix.at[at], joined.at[at], mask_x, True)
        back = norm_backward(
            ax[at].astype(F32), c.astype(F32), rstd_x[h], gx, joined.at[at], fwx, dn.at[at]
        )
        outs[h] = back.reshape(outs.shape[1:])
        tr_begin(2 + h)
        keep = pltpu.make_async_copy(outs.at[h, :, :, me], out.at[:, me, h], local.at[6 + h])
        keep.start()
        kept.append(keep)

    for k in ks:
        for s in range(2):
            role0(s, k).wait_send()
            role1(s, k).wait_send()
            role2(s, k).wait_send()
            role5(s, k).wait_send()
        role3(k).wait_send()
        role4(k).wait_send()
    for h in range(parts):
        tr_end(2 + h)
        kept[h].wait()


DIRECT = (2, 2, 3, 3)
TOK_AFTER = 1


def fits_kernel(trs, gzs, slab, y, x_own, width, depth):
    return (trs, gzs, y, x_own) == (4, 8, 32, 2) and (slab * trs * x_own * 4) % 32 == 0 and width % 128 == 0 and depth % 64 == 0


def fused(trs, gzs, tokens, cotangent, gain_x, wqkv_x, wo_x, gain_z, wqkv_z, wo_z):
    slab, y, x_own, width = tokens.shape
    x, z = x_own * trs, slab * gzs
    rows = slab * y * x_own
    parts, group = 2, gzs // 2
    split = (slab, trs, parts, group, x_own, width)
    block = rows // 4
    lines = (slab, group, 2, trs // 2, x_own, width)
    vm = pl.BlockSpec(memory_space=pltpu.VMEM)
    hbm = pl.BlockSpec(memory_space=pl.ANY)
    wide = wqkv_x.shape[1]
    result = pl.pallas_call(
        functools.partial(kernel, trs, gzs, x),
        out_shape=jax.ShapeDtypeStruct(split, BF16),
        in_specs=[hbm, hbm, vm, hbm, hbm, vm, hbm, hbm],
        out_specs=hbm,
        scratch_shapes=[
            pltpu.VMEM((slab, parts, group, trs, x_own, width), BF16),
            pltpu.VMEM((slab, parts, group, 2, trs // 2, x_own, width), BF16),
            pltpu.VMEM((z, parts, 2, x_own, width), BF16),
            pltpu.VMEM((parts, *lines), BF16),
            pltpu.VMEM((parts, z, 2, x_own, width), BF16),
            pltpu.VMEM((parts, z, 2, x_own, width), BF16),
            pltpu.VMEM((parts, *lines), BF16),
            pltpu.VMEM((parts, slab, group, trs, x_own, width), BF16),
        ]
        + [pltpu.VMEM((width, wide), BF16), pltpu.VMEM((width, width), BF16)] * 2
        + [pltpu.VMEM((rows, wide), BF16)] * 2
        + [pltpu.VMEM((4 * H, block, block), F32)]
        + [pltpu.VMEM((rows, width), BF16)] * 2
        + [pltpu.VMEM((rows, wide), BF16), pltpu.VMEM((rows, width), F32)]
        + [pltpu.VMEM((rows, width), BF16)] * 3
        + [
            pltpu.SemaphoreType.DMA((4, trs)),
            pltpu.SemaphoreType.DMA((4, trs)),
            pltpu.SemaphoreType.DMA((5, gzs)),
            pltpu.SemaphoreType.DMA((5, gzs)),
            pltpu.SemaphoreType.DMA((2, 4, 6)),
            pltpu.SemaphoreType.DMA((2, 4, 6)),
            pltpu.SemaphoreType.DMA((8,)),
        ],
        compiler_params=pltpu.CompilerParams(
            collective_id=0, has_side_effects=True, vmem_limit_bytes=56 * 1024 * 1024
        ),
    )(
        tokens.reshape(split), cotangent.reshape(split),
        gain_x, wqkv_x, wo_x, gain_z, wqkv_z, wo_z,
    )
    return result.reshape(tokens.shape)


def solution(mesh):
    trs, gzs = mesh.shape["tr"], mesh.shape["gz"]

    def body(tokens, *rest):
        if fits_kernel(trs, gzs, *tokens.shape, rest[2].shape[0]):
            return fused(trs, gzs, tokens, *rest)
        return per_device(tokens, *rest)

    return jax.shard_map(
        body,
        mesh=mesh,
        in_specs=(
            P("gz", None, "tr", None),
            P("gz", None, "tr", None),
            P(),
            P("tr", None),
            P("tr", None),
            P(),
            P("tr", None),
            P("tr", None),
        ),
        out_specs=P("gz", None, "tr", None),
        check_vma=False,
    )
```

```python
import functools
import math

import jax
import jax.numpy as jnp
import numpy as np
from jax import lax
from jax.experimental import pallas as pl
from jax.experimental.pallas import tpu as pltpu
from jax.sharding import PartitionSpec as P

H = 6


def head_split(packed, index, model_width):
    piece = packed[..., index * model_width : (index + 1) * model_width]
    return piece.reshape(piece.shape[:-1] + (H, model_width // H))


def merge_heads(value):
    return value.reshape(value.shape[:-2] + (value.shape[-2] * value.shape[-1],))


def recompute(tokens_in, gain_vec, w_in, layout):
    model_width = w_in.shape[0]
    factor = 1.0 / math.sqrt(model_width // H)
    widened = tokens_in.astype(jnp.float32)
    inv_rms = lax.rsqrt(jnp.mean(widened * widened, axis=-1, keepdims=True) + 1e-06)
    normed = (widened * inv_rms * gain_vec).astype(jnp.bfloat16)
    packed = jnp.dot(normed, w_in, preferred_element_type=jnp.float32).astype(jnp.bfloat16)
    queries = head_split(packed, 0, model_width)
    key_part = head_split(packed, 1, model_width)
    values = head_split(packed, 2, model_width)
    key_form = layout.replace("l", "m")
    scores = (
        jnp.einsum(
            layout + "," + key_form + "->bhlm",
            queries,
            key_part,
            preferred_element_type=jnp.float32,
        )
        * factor
    )
    highest = jnp.max(scores, axis=-1, keepdims=True)
    expanded = jnp.exp(scores - highest)
    probs = expanded / jnp.sum(expanded, axis=-1, keepdims=True)
    return (widened, inv_rms, queries, key_part, values, probs, probs.astype(jnp.bfloat16), factor)


def forward_out(tokens_in, gain_vec, w_in, w_out, layout):
    widened, inv_rms, queries, key_part, values, probs, probs_b, factor = recompute(
        tokens_in, gain_vec, w_in, layout
    )
    key_form = layout.replace("l", "m")
    mixed = jnp.einsum(
        "bhlm," + key_form + "->" + layout, probs_b, values, preferred_element_type=jnp.float32
    )
    mixed = merge_heads(mixed.astype(jnp.bfloat16))
    return (widened + jnp.dot(mixed, w_out, preferred_element_type=jnp.float32)).astype(
        jnp.bfloat16
    )


def backward(tokens_in, upstream, gain_vec, w_in, w_out, layout):
    widened, inv_rms, queries, key_part, values, probs, probs_b, factor = recompute(
        tokens_in, gain_vec, w_in, layout
    )
    key_form = layout.replace("l", "m")
    d_mixed = jnp.dot(upstream, w_out.T, preferred_element_type=jnp.float32).astype(jnp.bfloat16)
    d_mixed = d_mixed.reshape(d_mixed.shape[:-1] + (H, d_mixed.shape[-1] // H))
    d_probs = jnp.einsum(
        layout + "," + key_form + "->bhlm", d_mixed, values, preferred_element_type=jnp.float32
    )
    d_values = jnp.einsum(
        "bhlm," + layout + "->" + key_form, probs_b, d_mixed, preferred_element_type=jnp.float32
    ).astype(jnp.bfloat16)
    centre = jnp.sum(probs * d_probs, axis=-1, keepdims=True)
    d_scores = (probs * (d_probs - centre) * factor).astype(jnp.bfloat16)
    d_queries = jnp.einsum(
        "bhlm," + key_form + "->" + layout, d_scores, key_part, preferred_element_type=jnp.float32
    ).astype(jnp.bfloat16)
    d_keys = jnp.einsum(
        "bhlm," + layout + "->" + key_form, d_scores, queries, preferred_element_type=jnp.float32
    ).astype(jnp.bfloat16)
    joined = jnp.concatenate(
        [merge_heads(d_queries), merge_heads(d_keys), merge_heads(d_values)], axis=-1
    )
    d_normed = jnp.dot(joined, w_in.T, preferred_element_type=jnp.float32)
    scaled = d_normed * gain_vec
    d_tokens = inv_rms * (
        scaled - widened * inv_rms * inv_rms * jnp.mean(scaled * widened, axis=-1, keepdims=True)
    )
    return (upstream.astype(jnp.float32) + d_tokens).astype(jnp.bfloat16)


def line_forward(lines, gain_vec, w_in, w_out):
    feature_count = lines.shape[3]
    flat = lines.reshape(-1, lines.shape[2], feature_count)
    return forward_out(flat, gain_vec, w_in, w_out, "blhe").reshape(lines.shape)


def line_backward(lines, upstream, gain_vec, w_in, w_out):
    feature_count = lines.shape[3]
    flat = lines.reshape(-1, lines.shape[2], feature_count)
    flat_up = upstream.reshape(flat.shape)
    return backward(flat, flat_up, gain_vec, w_in, w_out, "blhe").reshape(lines.shape)


def per_device(tokens, cotangent, gain_x, wqkv_x, wo_x, gain_z, wqkv_z, wo_z):
    full_in_x, full_out_x = (
        lax.all_gather(wqkv_x, "tr", axis=0, tiled=True),
        lax.all_gather(wo_x, "tr", axis=0, tiled=True),
    )
    full_in_z, full_out_z = (
        lax.all_gather(wqkv_z, "tr", axis=0, tiled=True),
        lax.all_gather(wo_z, "tr", axis=0, tiled=True),
    )
    width = tokens.shape[-1]
    lines = lax.all_to_all(tokens, "tr", split_axis=1, concat_axis=2, tiled=True)
    cot_lines = lax.all_to_all(cotangent, "tr", split_axis=1, concat_axis=2, tiled=True)
    cells = lines.shape[1] * lines.shape[2]
    flat = (lines.shape[0], cells, width)
    cot_columns = lax.all_to_all(
        cot_lines.reshape(flat), "gz", split_axis=1, concat_axis=0, tiled=True
    )
    mid_lines = line_forward(lines, gain_x, full_in_x, full_out_x)
    mid_columns = lax.all_to_all(
        mid_lines.reshape(flat), "gz", split_axis=1, concat_axis=0, tiled=True
    )
    grad_columns = backward(
        mid_columns, cot_columns, gain_z, full_in_z, full_out_z, "lbhe"
    )
    grad_lines = lax.all_to_all(grad_columns, "gz", split_axis=0, concat_axis=1, tiled=True)
    result_lines = line_backward(lines, grad_lines.reshape(lines.shape), gain_x, full_in_x, full_out_x)
    return lax.all_to_all(result_lines, "tr", split_axis=2, concat_axis=1, tiled=True)


F32, BF16 = jnp.float32, jnp.bfloat16


def nt(a, b):
    return lax.dot_general(a, b, (((1,), (1,)), ((), ())), preferred_element_type=F32)


def tn(a, b):
    return lax.dot_general(a, b, (((0,), (0,)), ((), ())), preferred_element_type=F32)


def nn(a, b):
    return jnp.dot(a, b, preferred_element_type=F32)


def rms(a):
    return lax.rsqrt(jnp.mean(a * a, axis=-1, keepdims=True) + 1e-06)


def project(a, rstd, gain, w, qkv):
    width = a.shape[1]
    normed = (a * rstd * gain).astype(BF16)
    for j in range(3):
        cols = slice(j * width, (j + 1) * width)
        qkv[:, cols] = nn(normed, w[:, cols]).astype(BF16)


def line_mask(block, line, inner):
    key = lax.broadcasted_iota(jnp.int32, (block, block), 0)
    query = lax.broadcasted_iota(jnp.int32, (block, block), 1)
    if inner:
        return key % line == query % line
    return key // line == query // line


def head_spans(width):
    size = width // H
    return [[pl.ds(n * width + h * size, size) for n in range(3)] for h in range(H)]


def softmax_rows(qkv, at, spans, mask, factor):
    qk = [nt(qkv[at, sp[1]], qkv[at, sp[0]]) for sp in spans]
    scores = [jnp.where(mask, x * factor, -1e30) for x in qk]
    tops = [jnp.max(x, axis=0, keepdims=True) for x in scores]
    grown = [jnp.exp(x - t) for x, t in zip(scores, tops)]
    sums = [1.0 / jnp.sum(x, axis=0, keepdims=True) for x in grown]
    return [x * t for x, t in zip(grown, sums)]


def attend_scores(qkv, probs, first, mask):
    rows = qkv.shape[0]
    width = qkv.shape[1] // 3
    block = mask.shape[0]
    factor = 1.0 / math.sqrt(width // H)
    for b in range(rows // block):
        ps = softmax_rows(qkv, pl.ds(b * block, block), head_spans(width), mask, factor)
        for h, p in enumerate(ps):
            probs[(first + b) * H + h] = p


def attend_forward(qkv, probs, first, mixed, mask):
    rows, width = mixed.shape
    block = mask.shape[0]
    factor = 1.0 / math.sqrt(width // H)
    spans = head_spans(width)
    for b in range(rows // block):
        at = pl.ds(b * block, block)
        ps = softmax_rows(qkv, at, spans, mask, factor)
        for h, p in enumerate(ps):
            probs[(first + b) * H + h] = p
        outs = [tn(p.astype(BF16), qkv[at, sp[2]]) for p, sp in zip(ps, spans)]
        for sp, o in zip(spans, outs):
            mixed[at, sp[0]] = o.astype(BF16)


def attend_backward(qkv, probs, first, d_mixed, joined):
    rows, width = d_mixed.shape
    block = probs.shape[1]
    factor = 1.0 / math.sqrt(width // H)
    spans = head_spans(width)
    for b in range(rows // block):
        at = pl.ds(b * block, block)
        dps = [nt(qkv[at, sp[2]], d_mixed[at, sp[0]]) for sp in spans]
        ps = [probs[(first + b) * H + h] for h in range(H)]
        dvs = [nn(p.astype(BF16), d_mixed[at, sp[0]]) for p, sp in zip(ps, spans)]
        centres = [jnp.sum(p * dp, axis=0, keepdims=True) for p, dp in zip(ps, dps)]
        dss = [(p * (dp - c) * factor).astype(BF16) for p, dp, c in zip(ps, dps, centres)]
        dks = [nn(ds, qkv[at, sp[0]]) for ds, sp in zip(dss, spans)]
        dqs = [tn(ds, qkv[at, sp[1]]) for ds, sp in zip(dss, spans)]
        for sp, dq, dk, dv in zip(spans, dqs, dks, dvs):
            joined[at, sp[0]] = dq.astype(BF16)
            joined[at, sp[1]] = dk.astype(BF16)
            joined[at, sp[2]] = dv.astype(BF16)


def norm_backward(a, c, rstd, gain, joined, w, dn):
    width = a.shape[-1]
    part = width // 3
    for j in range(3):
        dn[:, j * part : (j + 1) * part] = nt(joined[...], w[j * part : (j + 1) * part, :])
    scaled = dn[...] * gain
    mean = jnp.mean(scaled * a, axis=-1, keepdims=True)
    return (c + rstd * (scaled - a * (rstd * rstd) * mean)).astype(BF16)


def kernel(
    nt_, ng, line_x,
    tok, cot, gain_x, wx, ox, gain_z, wz, oz, out,
    tokr, cotz, mids, midr, grads, gradr, outs,
    fwx, fox, fwz, foz, qkvx, qkvz, probs, probz, mixed, dmix, joined, dn, ax, az, cz,
    tr_send, tr_recv, gz_send, gz_recv, w_send, w_recv, c_send, c_recv, entered, local,
):
    me, mine = lax.axis_index("tr"), lax.axis_index("gz")
    sib, across = me + 1 - 2 * (me % 2), (me + 2) % nt_
    gy, gp = mine % 2, (mine // 2) % 2
    ynbr, znbr = mine + 1 - 2 * gy, mine + 2 - 4 * gp
    slab, pairs, width = tok.shape[0], tok.shape[3], tok.shape[5]
    parts = tok.shape[2]
    half = ax.shape[0] // parts
    block = half // 2

    def tell(sem, t, g):
        pl.semaphore_signal(sem, inc=1, device_id=(t, g), device_id_type=pl.DeviceIdType.MESH)

    zrow, last = mine // 2, ng // 2 - 1

    def tell_lanes(sem):
        for d in range(1, nt_):
            tell(sem, (me + d) % nt_, mine)

    def tell_near(sem):
        tell(sem, me, ynbr)
        pl.when(zrow > 0)(lambda: tell(sem, me, mine - 2))
        pl.when(zrow < last)(lambda: tell(sem, me, mine + 2))

    near = 1 + (zrow + last) // (last + 1) + (2 * last - zrow) // (last + 1)

    barrier = pltpu.get_barrier_semaphore()
    tell_lanes(barrier)
    if NEAR:
        tell_near(barrier)
    else:
        for d in range(1, ng):
            tell(barrier, me, (mine + d) % ng)

    own_w = ((wx, wx, wx, ox), (wz, wz, wz, oz))
    full_w = ((fwx, fwx, fwx, fox), (fwz, fwz, fwz, foz))
    depth = wx.shape[0]
    quarter = depth // 4

    here = [
        pltpu.make_async_copy(tok.at[:, me], tokr.at[:, :, :, me], local.at[0]),
    ]
    for s in range(2):
        for k in (0, 3):
            to = full_w[s][k].at[pl.ds(pl.multiple_of(me * depth, 16), depth)]
            here.append(pltpu.make_async_copy(own_w[s][k], to, local.at[len(here)]))
    for copy in here:
        copy.start()

    if NEAR:
        pl.semaphore_wait(barrier, nt_ - 1 + near)
        tell_near(entered.at[0])
    else:
        pl.semaphore_wait(barrier, nt_ + ng - 2)
        tell_lanes(entered.at[3])

    def widen(step):
        if step < 3:
            if NEAR:
                pl.semaphore_wait(entered.at[step], near)
                if step < 2:
                    tell_near(entered.at[step + 1])
                else:
                    tell_lanes(entered.at[3])
        else:
            pl.semaphore_wait(entered.at[3], nt_ - 1)

    def remote(src, dst, send, recv, t, g):
        return pltpu.make_async_remote_copy(
            src_ref=src, dst_ref=dst, send_sem=send, recv_sem=recv,
            device_id=(t, g), device_id_type=pl.DeviceIdType.MESH,
        )

    def own(s, k, row, n):
        at = pl.ds(pl.multiple_of(row, 16), n)
        return own_w[s][k].at[at, pl.ds((k % 3) * width, width)]

    def spot(s, k, shard, row, n):
        at = pl.ds(pl.multiple_of(shard * depth + row, 16), n)
        return full_w[s][k].at[at, pl.ds((k % 3) * width, width)]

    def push(s, k, role, src, dst, t, g):
        return remote(src, dst, w_send.at[s, k, role], w_recv.at[s, k, role], t, g)

    odd = (gy + gp) % 2
    q_me, q_d = (2 * odd + gy) * quarter, (2 * odd + 1 - gy) * quarter
    q_y, q_z = (3 - 2 * odd - gy) * quarter, (2 - 2 * odd + gy) * quarter
    by_z = (0, 1)

    def direct_rows(s, k):
        if s == 0 or DIRECT[k] == 0:
            return q_me, quarter
        if DIRECT[k] == 1:
            return 2 * odd * quarter, 2 * quarter
        n = DIRECT[k] * quarter
        return gy * (depth - n), n

    def relay_rows(s, k, sent):
        if s == 0 or DIRECT[k] <= 1:
            return (q_me if sent else q_y), quarter
        n = DIRECT[k] * quarter
        return (gy if sent else 1 - gy) * n, depth - n

    def over_z(s, k):
        return s == 0 or DIRECT[k] <= 1

    def role0(s, k):
        row, n = direct_rows(s, k)
        return push(s, k, 0, own(s, k, row, n), spot(s, k, me, row, n), across, mine)

    def role1(s, k):
        return push(s, k, 1, own(s, k, 0, depth), spot(s, k, me, 0, depth), sib, mine)

    def role2(s, k):
        row, n = relay_rows(s, k, True)
        at = spot(s, k, across, row, n)
        return push(s, k, 2, at, at, me, ynbr)

    def role3(s, k):
        at = spot(s, k, across, q_me, quarter)
        return push(s, k, 3, at, at, me, znbr)

    def role4(s, k):
        if k in by_z:
            at = spot(s, k, across, q_y, quarter)
            return push(s, k, 4, at, at, me, znbr)
        at = spot(s, k, across, q_z, quarter)
        return push(s, k, 4, at, at, me, ynbr)

    def two_steps(s, k):
        return s == 0 or DIRECT[k] == 0

    def role5(s, k):
        at = spot(s, k, across, 0, depth)
        return push(s, k, 5, at, at, sib, mine)

    def arrived(s, k, role):
        if role == 0:
            at = spot(s, k, across, *direct_rows(s, k))
        elif role == 1:
            at = spot(s, k, sib, 0, depth)
        elif role == 2:
            at = spot(s, k, across, *relay_rows(s, k, False))
        elif role == 3:
            at = spot(s, k, across, q_z, quarter)
        elif role == 4:
            at = spot(s, k, across, q_d, quarter)
        else:
            at = spot(s, k, (sib + 2) % nt_, 0, depth)
        push(s, k, role, at, at, sib, mine).wait_recv()

    def tr_copy(n, d):
        t = (me + d) % nt_
        src, dst = tr_ends(n, t, me)
        return remote(src, dst, tr_send.at[n, d], tr_recv.at[n, d], t, mine)

    def tr_ends(n, to, source):
        if n == 0:
            return tok.at[:, to], tokr.at[:, :, :, source]
        return outs.at[n - 1, :, :, to], out.at[:, source, n - 1]

    def gz_ends(n, to, source):
        if n < 2:
            h = n
            return mids.at[h, :, to // 2, :, to % 2], midr.at[h, pl.ds(source * slab, slab)]
        h = n - 2
        return grads.at[h, pl.ds(to * slab, slab)], gradr.at[h, :, source // 2, :, source % 2]

    def gz_copy(n, d):
        g = (mine + d) % ng
        src, dst = gz_ends(n, g, mine)
        return remote(src, dst, gz_send.at[n, d], gz_recv.at[n, d], me, g)

    far_first = [2, 3, 1] if nt_ == 4 else list(range(1, nt_))
    gz_order = sorted(range(1, ng), key=lambda d: -min(d, ng - d))

    def tr_begin(n):
        for d in far_first:
            tr_copy(n, d).start()

    def tr_end(n):
        for d in range(1, nt_):
            tr_copy(n, d).wait_send()
            src = (me + nt_ - d) % nt_
            at = tr_ends(n, me, src)[1]
            remote(at, at, tr_send.at[n, d], tr_recv.at[n, d], src, mine).wait_recv()

    def gz_begin(n):
        for d in gz_order:
            gz_copy(n, d).start()

    def gz_end(n):
        for d in range(1, ng):
            gz_copy(n, d).wait_send()
            src = (mine + ng - d) % ng
            at = gz_ends(n, mine, src)[1]
            remote(at, at, gz_send.at[n, d], gz_recv.at[n, d], me, src).wait_recv()

    core, zc, zs = me % 2, mine // 2, ng // 2
    lanes = (me, sib, across, (sib + 2) % nt_)

    def cot_copy(j, dz, only_at=None):
        z = (zc + dz) % zs
        src = cot.at[:, lanes[j], :, z]
        dst = cotz.at[pl.ds(mine * slab, slab), :, me // 2]
        return remote(src, dst, c_send.at[j, dz], c_recv.at[j, dz, gy], lanes[j], 2 * z + core)

    def unless_self(j, dz, test, act):
        if j == 0 and dz == 0:
            pl.when(test)(act)
        else:
            act()

    def cot_begin(js):
        for dz in (2, 1, 3, 0):
            for j in js:
                unless_self(j, dz, core != gy, lambda: cot_copy(j, dz).start())

    def cot_end():
        for dz in range(zs):
            for j in range(4):
                unless_self(j, dz, core != gy, lambda: cot_copy(j, dz).wait_send())
        other = (core + gy) % 2
        for i in range(2):
            at_x = (me // 2 + i) % 2
            for dz in range(zs):
                for ys in range(2):
                    g = 2 * ((zc + zs - dz) % zs) + ys
                    at = cotz.at[pl.ds(g * slab, slab), :, at_x]
                    copy = remote(at, at, c_send.at[0, 0], c_recv.at[other + 2 * i, dz, ys], sib, mine)
                    if i == 0 and dz == 0:
                        pl.when((core != gy) | (gy != ys))(lambda: copy.wait_recv())
                    else:
                        copy.wait_recv()
        pl.when(core == gy)(lambda: cot_self().wait())

    def cot_self():
        return pltpu.make_async_copy(cot.at[:, me, :, zc], cotz.at[pl.ds(mine * slab, slab), :, me // 2], local.at[7])

    ks = range(4)

    def begin_w1(pieces):
        for k in pieces:
            role0(1, k).start()

    for k in ks:
        role0(0, k).start()
    for k in ks:
        role1(0, k).start()
    pl.when(core == gy)(lambda: cot_self().start())
    for step in range(3):
        widen(step)
    if COT0 == 0:
        cot_begin((0,))
    if WIDE == 0:
        widen(3)
        cot_begin((1,))
    for k in ks:
        arrived(0, k, 0)
        role2(0, k).start()
        role3(0, k).start()
        if k == 0 and WIDE == 1:
            widen(3)
            if COT0 == 0:
                cot_begin((1,))
        if k == TOK_AFTER:
            tr_begin(0)
        begin_w1([j for j in ks if W1_AT[j] == k])
        if COT1 == k:
            cot_begin((2, 3))
    for k in ks:
        arrived(0, k, 2)
        if k in by_z:
            role4(0, k).start()
        arrived(0, k, 3)
        if k not in by_z:
            role4(0, k).start()
    if COT0 == 4:
        cot_begin((0, 1))
    begin_w1([j for j in ks if W1_AT[j] == 4])
    if COT1 == 4:
        cot_begin((2, 3))
    for k in ks:
        arrived(0, k, 4)
        role5(0, k).start()
    for copy in here:
        copy.wait()
    tr_end(0)
    begin_w1([j for j in ks if W1_AT[j] == 5])
    if COT1 == 5:
        cot_begin((2, 3))
    for k in ks:
        role1(1, k).start()
    for h in range(parts):
        ax[pl.ds(h * half, half)] = tokr[:, h].reshape(half, width)
    for k in ks:
        arrived(0, k, 1)
        arrived(0, k, 5)

    def relay_z(pieces):
        for k in pieces:
            arrived(1, k, 0)
            role2(1, k).start()
            if over_z(1, k):
                role3(1, k).start()

    mask_x = line_mask(block, line_x, False)
    mask_z = line_mask(block, block // (slab * ng), True)
    gx, gz = gain_x[...][None], gain_z[...][None]
    rstd_x = []
    for h in range(parts):
        at = pl.ds(h * half, half)
        a = ax[at].astype(F32)
        rstd_x.append(rms(a))
        project(a, rstd_x[h], gx, fwx, qkvx.at[at])
        attend_forward(qkvx.at[at], probs, 2 * h, mixed.at[at], mask_x)
        mid = ax[at].astype(F32) + nn(mixed[at], fox[...])
        mids[h] = mid.astype(BF16).reshape(mids.shape[1:])
        gz_begin(h)
        midr[h, pl.ds(mine * slab, slab)] = mids[h, :, mine // 2, :, mine % 2]
        if h == 0:
            relay_z(RELAY1)
    relay_z([k for k in ks if k not in RELAY1])
    for k in ks:
        arrived(1, k, 2)
        if over_z(1, k):
            arrived(1, k, 3)
        if two_steps(1, k):
            role4(1, k).start()
        else:
            role5(1, k).start()
    for k in ks:
        if two_steps(1, k):
            arrived(1, k, 4)
            role5(1, k).start()
    for k in ks:
        arrived(1, k, 1)
        arrived(1, k, 5)

    def z_front(h):
        at = pl.ds(h * half, half)
        gz_end(h)
        for j in range(2):
            az[pl.ds(h * half + j * block, block)] = midr[h, :, j].reshape(block, width)
        a = az[at].astype(F32)
        rstd = rms(a)
        project(a, rstd, gz, fwz, qkvz.at[at])
        attend_scores(qkvz.at[at], probz, 2 * h, mask_z)
        return rstd

    for h in range(parts):
        at = pl.ds(h * half, half)
        rstd = z_front(h)
        if h == 0:
            cot_end()
        for j in range(2):
            cz[pl.ds(h * half + j * block, block)] = cotz[:, h, j].reshape(block, width)
        dmix[at] = nt(cz[at], foz[...]).astype(BF16)
        attend_backward(qkvz.at[at], probz, 2 * h, dmix.at[at], joined.at[at])
        back = norm_backward(
            az[at].astype(F32), cz[at].astype(F32), rstd, gz, joined.at[at], fwz, dn.at[at]
        )
        for j in range(2):
            grads[h, :, j] = back[j * block : (j + 1) * block].reshape(slab * ng, block // (slab * ng), width)
        gz_begin(2 + h)
        gradr[h, :, mine // 2, :, mine % 2] = grads[h, pl.ds(mine * slab, slab)]

    kept = []
    for h in range(parts):
        at = pl.ds(h * half, half)
        gz_end(2 + h)
        c = gradr[h].reshape(half, width)
        dmix[at] = nt(c, fox[...]).astype(BF16)
        attend_backward(qkvx.at[at], probs, 2 * h, dmix.at[at], joined.at[at])
        back = norm_backward(
            ax[at].astype(F32), c.astype(F32), rstd_x[h], gx, joined.at[at], fwx, dn.at[at]
        )
        outs[h] = back.reshape(outs.shape[1:])
        tr_begin(1 + h)
        keep = pltpu.make_async_copy(outs.at[h, :, :, me], out.at[:, me, h], local.at[5 + h])
        keep.start()
        kept.append(keep)

    for k in ks:
        for s in range(2):
            role0(s, k).wait_send()
            role1(s, k).wait_send()
            role2(s, k).wait_send()
            role5(s, k).wait_send()
            if over_z(s, k):
                role3(s, k).wait_send()
            if two_steps(s, k):
                role4(s, k).wait_send()
    for h in range(parts):
        tr_end(1 + h)
        kept[h].wait()


DIRECT = (1, 1, 1, 1)
TOK_AFTER = 0
W1_AT = (3, 3, 3, 3)
COT0, COT1 = 0, 4
NEAR, WIDE = False, 0
RELAY1 = (0, 1)


def settle(given, out, held, came, went):
    count = given.shape[0]
    ins = [pltpu.make_async_copy(given.at[i], held.at[i], came.at[i]) for i in range(count)]
    outs = [pltpu.make_async_copy(held.at[i], out.at[i], went.at[i]) for i in range(count)]
    for copy in ins:
        copy.start()
    for a, b in zip(ins, outs):
        a.wait()
        b.start()
    for copy in outs:
        copy.wait()


def fits_kernel(trs, gzs, slab, y, x_own, width, depth):
    return (trs, gzs, y, x_own) == (4, 8, 32, 2) and (slab * trs * x_own * 4) % 32 == 0 and width % 128 == 0 and depth % 64 == 0


def fused(trs, gzs, tokens, cotangent, gain_x, wqkv_x, wo_x, gain_z, wqkv_z, wo_z):
    slab, y, x_own, width = tokens.shape
    x, z = x_own * trs, slab * gzs
    rows = slab * y * x_own
    parts, group = 2, gzs // 2
    split = (slab, trs, parts, group, x_own, width)
    block = rows // 4
    lines = (slab, group, 2, trs // 2, x_own, width)
    vm = pl.BlockSpec(memory_space=pltpu.VMEM)
    hbm = pl.BlockSpec(memory_space=pl.ANY)
    wide = wqkv_x.shape[1]
    result = pl.pallas_call(
        functools.partial(kernel, trs, gzs, x),
        out_shape=jax.ShapeDtypeStruct(split, BF16),
        in_specs=[hbm, hbm, vm, hbm, hbm, vm, hbm, hbm],
        out_specs=hbm,
        scratch_shapes=[
            pltpu.VMEM((slab, parts, group, trs, x_own, width), BF16),
            pltpu.VMEM((z, parts, 2, x_own, width), BF16),
            pltpu.VMEM((parts, *lines), BF16),
            pltpu.VMEM((parts, z, 2, x_own, width), BF16),
            pltpu.VMEM((parts, z, 2, x_own, width), BF16),
            pltpu.VMEM((parts, *lines), BF16),
            pltpu.VMEM((parts, slab, group, trs, x_own, width), BF16),
        ]
        + [pltpu.VMEM((width, wide), BF16), pltpu.VMEM((width, width), BF16)] * 2
        + [pltpu.VMEM((rows, wide), BF16)] * 2
        + [pltpu.VMEM((4 * H, block, block), F32)] * 2
        + [pltpu.VMEM((rows, width), BF16)] * 2
        + [pltpu.VMEM((rows, wide), BF16), pltpu.VMEM((rows, width), F32)]
        + [pltpu.VMEM((rows, width), BF16)] * 3
        + [
            pltpu.SemaphoreType.DMA((3, trs)),
            pltpu.SemaphoreType.DMA((3, trs)),
            pltpu.SemaphoreType.DMA((4, gzs)),
            pltpu.SemaphoreType.DMA((4, gzs)),
            pltpu.SemaphoreType.DMA((2, 4, 6)),
            pltpu.SemaphoreType.DMA((2, 4, 6)),
            pltpu.SemaphoreType.DMA((4, gzs // 2)),
            pltpu.SemaphoreType.DMA((4, gzs // 2, 2)),
            pltpu.SemaphoreType.REGULAR((4,)),
            pltpu.SemaphoreType.DMA((8,)),
        ],
        compiler_params=pltpu.CompilerParams(
            collective_id=0, has_side_effects=True, vmem_limit_bytes=56 * 1024 * 1024
        ),
    )(
        tokens.reshape(split), cotangent.reshape(split),
        gain_x, wqkv_x, wo_x, gain_z, wqkv_z, wo_z,
    )
    return pl.pallas_call(
        settle,
        out_shape=jax.ShapeDtypeStruct(tokens.shape, BF16),
        in_specs=[hbm],
        out_specs=hbm,
        scratch_shapes=[
            pltpu.VMEM(tokens.shape, BF16),
            pltpu.SemaphoreType.DMA((slab,)),
            pltpu.SemaphoreType.DMA((slab,)),
        ],
    )(result.reshape(tokens.shape))


def solution(mesh):
    trs, gzs = mesh.shape["tr"], mesh.shape["gz"]

    def body(tokens, *rest):
        if fits_kernel(trs, gzs, *tokens.shape, rest[2].shape[0]):
            return fused(trs, gzs, tokens, *rest)
        return per_device(tokens, *rest)

    return jax.shard_map(
        body,
        mesh=mesh,
        in_specs=(
            P("gz", None, "tr", None),
            P("gz", None, "tr", None),
            P(),
            P("tr", None),
            P("tr", None),
            P(),
            P("tr", None),
            P("tr", None),
        ),
        out_specs=P("gz", None, "tr", None),
        check_vma=False,
    )
```

```python
import functools
import math

import jax
import jax.numpy as jnp
import numpy as np
from jax import lax
from jax.experimental import pallas as pl
from jax.experimental.pallas import tpu as pltpu
from jax.sharding import PartitionSpec as P

H = 6


def head_split(packed, index, model_width):
    piece = packed[..., index * model_width : (index + 1) * model_width]
    return piece.reshape(piece.shape[:-1] + (H, model_width // H))


def merge_heads(value):
    return value.reshape(value.shape[:-2] + (value.shape[-2] * value.shape[-1],))


def recompute(tokens_in, gain_vec, w_in, layout):
    model_width = w_in.shape[0]
    factor = 1.0 / math.sqrt(model_width // H)
    widened = tokens_in.astype(jnp.float32)
    inv_rms = lax.rsqrt(jnp.mean(widened * widened, axis=-1, keepdims=True) + 1e-06)
    normed = (widened * inv_rms * gain_vec).astype(jnp.bfloat16)
    packed = jnp.dot(normed, w_in, preferred_element_type=jnp.float32).astype(jnp.bfloat16)
    queries = head_split(packed, 0, model_width)
    key_part = head_split(packed, 1, model_width)
    values = head_split(packed, 2, model_width)
    key_form = layout.replace("l", "m")
    scores = (
        jnp.einsum(
            layout + "," + key_form + "->bhlm",
            queries,
            key_part,
            preferred_element_type=jnp.float32,
        )
        * factor
    )
    highest = jnp.max(scores, axis=-1, keepdims=True)
    expanded = jnp.exp(scores - highest)
    probs = expanded / jnp.sum(expanded, axis=-1, keepdims=True)
    return (widened, inv_rms, queries, key_part, values, probs, probs.astype(jnp.bfloat16), factor)


def forward_out(tokens_in, gain_vec, w_in, w_out, layout):
    widened, inv_rms, queries, key_part, values, probs, probs_b, factor = recompute(
        tokens_in, gain_vec, w_in, layout
    )
    key_form = layout.replace("l", "m")
    mixed = jnp.einsum(
        "bhlm," + key_form + "->" + layout, probs_b, values, preferred_element_type=jnp.float32
    )
    mixed = merge_heads(mixed.astype(jnp.bfloat16))
    return (widened + jnp.dot(mixed, w_out, preferred_element_type=jnp.float32)).astype(
        jnp.bfloat16
    )


def backward(tokens_in, upstream, gain_vec, w_in, w_out, layout):
    widened, inv_rms, queries, key_part, values, probs, probs_b, factor = recompute(
        tokens_in, gain_vec, w_in, layout
    )
    key_form = layout.replace("l", "m")
    d_mixed = jnp.dot(upstream, w_out.T, preferred_element_type=jnp.float32).astype(jnp.bfloat16)
    d_mixed = d_mixed.reshape(d_mixed.shape[:-1] + (H, d_mixed.shape[-1] // H))
    d_probs = jnp.einsum(
        layout + "," + key_form + "->bhlm", d_mixed, values, preferred_element_type=jnp.float32
    )
    d_values = jnp.einsum(
        "bhlm," + layout + "->" + key_form, probs_b, d_mixed, preferred_element_type=jnp.float32
    ).astype(jnp.bfloat16)
    centre = jnp.sum(probs * d_probs, axis=-1, keepdims=True)
    d_scores = (probs * (d_probs - centre) * factor).astype(jnp.bfloat16)
    d_queries = jnp.einsum(
        "bhlm," + key_form + "->" + layout, d_scores, key_part, preferred_element_type=jnp.float32
    ).astype(jnp.bfloat16)
    d_keys = jnp.einsum(
        "bhlm," + layout + "->" + key_form, d_scores, queries, preferred_element_type=jnp.float32
    ).astype(jnp.bfloat16)
    joined = jnp.concatenate(
        [merge_heads(d_queries), merge_heads(d_keys), merge_heads(d_values)], axis=-1
    )
    d_normed = jnp.dot(joined, w_in.T, preferred_element_type=jnp.float32)
    scaled = d_normed * gain_vec
    d_tokens = inv_rms * (
        scaled - widened * inv_rms * inv_rms * jnp.mean(scaled * widened, axis=-1, keepdims=True)
    )
    return (upstream.astype(jnp.float32) + d_tokens).astype(jnp.bfloat16)


def line_forward(lines, gain_vec, w_in, w_out):
    feature_count = lines.shape[3]
    flat = lines.reshape(-1, lines.shape[2], feature_count)
    return forward_out(flat, gain_vec, w_in, w_out, "blhe").reshape(lines.shape)


def line_backward(lines, upstream, gain_vec, w_in, w_out):
    feature_count = lines.shape[3]
    flat = lines.reshape(-1, lines.shape[2], feature_count)
    flat_up = upstream.reshape(flat.shape)
    return backward(flat, flat_up, gain_vec, w_in, w_out, "blhe").reshape(lines.shape)


def per_device(tokens, cotangent, gain_x, wqkv_x, wo_x, gain_z, wqkv_z, wo_z):
    full_in_x, full_out_x = (
        lax.all_gather(wqkv_x, "tr", axis=0, tiled=True),
        lax.all_gather(wo_x, "tr", axis=0, tiled=True),
    )
    full_in_z, full_out_z = (
        lax.all_gather(wqkv_z, "tr", axis=0, tiled=True),
        lax.all_gather(wo_z, "tr", axis=0, tiled=True),
    )
    width = tokens.shape[-1]
    lines = lax.all_to_all(tokens, "tr", split_axis=1, concat_axis=2, tiled=True)
    cot_lines = lax.all_to_all(cotangent, "tr", split_axis=1, concat_axis=2, tiled=True)
    cells = lines.shape[1] * lines.shape[2]
    flat = (lines.shape[0], cells, width)
    cot_columns = lax.all_to_all(
        cot_lines.reshape(flat), "gz", split_axis=1, concat_axis=0, tiled=True
    )
    mid_lines = line_forward(lines, gain_x, full_in_x, full_out_x)
    mid_columns = lax.all_to_all(
        mid_lines.reshape(flat), "gz", split_axis=1, concat_axis=0, tiled=True
    )
    grad_columns = backward(
        mid_columns, cot_columns, gain_z, full_in_z, full_out_z, "lbhe"
    )
    grad_lines = lax.all_to_all(grad_columns, "gz", split_axis=0, concat_axis=1, tiled=True)
    result_lines = line_backward(lines, grad_lines.reshape(lines.shape), gain_x, full_in_x, full_out_x)
    return lax.all_to_all(result_lines, "tr", split_axis=2, concat_axis=1, tiled=True)


F32, BF16 = jnp.float32, jnp.bfloat16


def nt(a, b):
    return lax.dot_general(a, b, (((1,), (1,)), ((), ())), preferred_element_type=F32)


def tn(a, b):
    return lax.dot_general(a, b, (((0,), (0,)), ((), ())), preferred_element_type=F32)


def nn(a, b):
    return jnp.dot(a, b, preferred_element_type=F32)


def rms(a):
    return lax.rsqrt(jnp.mean(a * a, axis=-1, keepdims=True) + 1e-06)


def project(a, rstd, gain, w, qkv):
    width = a.shape[1]
    normed = (a * rstd * gain).astype(BF16)
    for j in range(3):
        cols = slice(j * width, (j + 1) * width)
        qkv[:, cols] = nn(normed, w[:, cols]).astype(BF16)


def line_mask(block, line, inner):
    key = lax.broadcasted_iota(jnp.int32, (block, block), 0)
    query = lax.broadcasted_iota(jnp.int32, (block, block), 1)
    if inner:
        return key % line == query % line
    return key // line == query // line


def head_spans(width):
    size = width // H
    return [[pl.ds(n * width + h * size, size) for n in range(3)] for h in range(H)]


def softmax_rows(qkv, at, spans, mask, factor):
    qk = [nt(qkv[at, sp[1]], qkv[at, sp[0]]) for sp in spans]
    scores = [jnp.where(mask, x * factor, -1e30) for x in qk]
    tops = [jnp.max(x, axis=0, keepdims=True) for x in scores]
    grown = [jnp.exp(x - t) for x, t in zip(scores, tops)]
    sums = [1.0 / jnp.sum(x, axis=0, keepdims=True) for x in grown]
    return [x * t for x, t in zip(grown, sums)]


def attend_scores(qkv, probs, first, mask):
    rows = qkv.shape[0]
    width = qkv.shape[1] // 3
    block = mask.shape[0]
    factor = 1.0 / math.sqrt(width // H)
    for b in range(rows // block):
        ps = softmax_rows(qkv, pl.ds(b * block, block), head_spans(width), mask, factor)
        for h, p in enumerate(ps):
            probs[(first + b) * H + h] = p


def attend_forward(qkv, probs, first, mixed, mask):
    rows, width = mixed.shape
    block = mask.shape[0]
    factor = 1.0 / math.sqrt(width // H)
    spans = head_spans(width)
    for b in range(rows // block):
        at = pl.ds(b * block, block)
        ps = softmax_rows(qkv, at, spans, mask, factor)
        for h, p in enumerate(ps):
            probs[(first + b) * H + h] = p
        outs = [tn(p.astype(BF16), qkv[at, sp[2]]) for p, sp in zip(ps, spans)]
        for sp, o in zip(spans, outs):
            mixed[at, sp[0]] = o.astype(BF16)


def attend_backward(qkv, probs, first, d_mixed, joined):
    rows, width = d_mixed.shape
    block = probs.shape[1]
    factor = 1.0 / math.sqrt(width // H)
    spans = head_spans(width)
    for b in range(rows // block):
        at = pl.ds(b * block, block)
        dps = [nt(qkv[at, sp[2]], d_mixed[at, sp[0]]) for sp in spans]
        ps = [probs[(first + b) * H + h] for h in range(H)]
        dvs = [nn(p.astype(BF16), d_mixed[at, sp[0]]) for p, sp in zip(ps, spans)]
        centres = [jnp.sum(p * dp, axis=0, keepdims=True) for p, dp in zip(ps, dps)]
        dss = [(p * (dp - c) * factor).astype(BF16) for p, dp, c in zip(ps, dps, centres)]
        dks = [nn(ds, qkv[at, sp[0]]) for ds, sp in zip(dss, spans)]
        dqs = [tn(ds, qkv[at, sp[1]]) for ds, sp in zip(dss, spans)]
        for sp, dq, dk, dv in zip(spans, dqs, dks, dvs):
            joined[at, sp[0]] = dq.astype(BF16)
            joined[at, sp[1]] = dk.astype(BF16)
            joined[at, sp[2]] = dv.astype(BF16)


def norm_backward(a, c, rstd, gain, joined, w, dn, turned):
    width = a.shape[-1]
    part = width // 3
    for j in range(3):
        cols = slice(j * part, (j + 1) * part)
        dn[:, cols] = nn(joined[...], w[:, cols]) if turned else nt(joined[...], w[cols, :])
    scaled = dn[...] * gain
    mean = jnp.mean(scaled * a, axis=-1, keepdims=True)
    return (c + rstd * (scaled - a * (rstd * rstd) * mean)).astype(BF16)


def kernel(
    nt_, ng, line_x,
    tok, cot, gain_x, wx, ox, gain_z, wz, oz, out,
    tokr, cotz, mids, midr, grads, gradr, outs,
    fwx, fox, fwz, foz, wxt, oxt, qkvx, qkvz, probs, probz, mixed, dmix, joined, dn, ax, az, cz,
    tr_send, tr_recv, gz_send, gz_recv, w_send, w_recv, c_send, c_recv, entered, local,
):
    me, mine = lax.axis_index("tr"), lax.axis_index("gz")
    sib, across = me + 1 - 2 * (me % 2), (me + 2) % nt_
    gy, gp = mine % 2, (mine // 2) % 2
    ynbr, znbr = mine + 1 - 2 * gy, mine + 2 - 4 * gp
    slab, pairs, width = tok.shape[0], tok.shape[3], tok.shape[5]
    parts = tok.shape[2]
    half = ax.shape[0] // parts
    block = half // 2

    def tell(sem, t, g):
        pl.semaphore_signal(sem, inc=1, device_id=(t, g), device_id_type=pl.DeviceIdType.MESH)

    zrow, last = mine // 2, ng // 2 - 1

    def tell_lanes(sem):
        for d in range(1, nt_):
            tell(sem, (me + d) % nt_, mine)

    def tell_near(sem):
        tell(sem, me, ynbr)
        pl.when(zrow > 0)(lambda: tell(sem, me, mine - 2))
        pl.when(zrow < last)(lambda: tell(sem, me, mine + 2))

    near = 1 + (zrow + last) // (last + 1) + (2 * last - zrow) // (last + 1)

    barrier = pltpu.get_barrier_semaphore()
    tell_lanes(barrier)
    if NEAR:
        tell_near(barrier)
    else:
        for d in range(1, ng):
            tell(barrier, me, (mine + d) % ng)

    own_w = ((wx, wx, wx, ox), (wz, wz, wz, oz))
    full_w = ((fwx, fwx, fwx, fox), (fwz, fwz, fwz, foz))
    depth = wx.shape[0]
    quarter = depth // 4

    here = [
        pltpu.make_async_copy(tok.at[:, me], tokr.at[:, :, :, me], local.at[0]),
    ]
    for s in range(2):
        for k in (0, 3):
            to = full_w[s][k].at[pl.ds(pl.multiple_of(me * depth, 16), depth)]
            here.append(pltpu.make_async_copy(own_w[s][k], to, local.at[len(here)]))
    for copy in here:
        copy.start()

    if NEAR:
        pl.semaphore_wait(barrier, nt_ - 1 + near)
        tell_near(entered.at[0])
    else:
        pl.semaphore_wait(barrier, nt_ + ng - 2)
        tell_lanes(entered.at[3])

    def widen(step):
        if step < 3:
            if NEAR:
                pl.semaphore_wait(entered.at[step], near)
                if step < 2:
                    tell_near(entered.at[step + 1])
                else:
                    tell_lanes(entered.at[3])
        else:
            pl.semaphore_wait(entered.at[3], nt_ - 1)

    def remote(src, dst, send, recv, t, g):
        return pltpu.make_async_remote_copy(
            src_ref=src, dst_ref=dst, send_sem=send, recv_sem=recv,
            device_id=(t, g), device_id_type=pl.DeviceIdType.MESH,
        )

    def own(s, k, row, n):
        at = pl.ds(pl.multiple_of(row, 16), n)
        return own_w[s][k].at[at, pl.ds((k % 3) * width, width)]

    def spot(s, k, shard, row, n):
        at = pl.ds(pl.multiple_of(shard * depth + row, 16), n)
        return full_w[s][k].at[at, pl.ds((k % 3) * width, width)]

    def push(s, k, role, src, dst, t, g):
        return remote(src, dst, w_send.at[s, k, role], w_recv.at[s, k, role], t, g)

    odd = (gy + gp) % 2
    q_me, q_d = (2 * odd + gy) * quarter, (2 * odd + 1 - gy) * quarter
    q_y, q_z = (3 - 2 * odd - gy) * quarter, (2 - 2 * odd + gy) * quarter
    by_z = (0, 1)

    def direct_rows(s, k):
        if s == 0 or DIRECT[k] == 0:
            return q_me, quarter
        if DIRECT[k] == 1:
            return 2 * odd * quarter, 2 * quarter
        n = DIRECT[k] * quarter
        return gy * (depth - n), n

    def relay_rows(s, k, sent):
        if s == 0 or DIRECT[k] <= 1:
            return (q_me if sent else q_y), quarter
        n = DIRECT[k] * quarter
        return (gy if sent else 1 - gy) * n, depth - n

    def over_z(s, k):
        return s == 0 or DIRECT[k] <= 1

    def role0(s, k):
        row, n = direct_rows(s, k)
        return push(s, k, 0, own(s, k, row, n), spot(s, k, me, row, n), across, mine)

    def role1(s, k):
        return push(s, k, 1, own(s, k, 0, depth), spot(s, k, me, 0, depth), sib, mine)

    def role2(s, k):
        row, n = relay_rows(s, k, True)
        at = spot(s, k, across, row, n)
        return push(s, k, 2, at, at, me, ynbr)

    def role3(s, k):
        at = spot(s, k, across, q_me, quarter)
        return push(s, k, 3, at, at, me, znbr)

    def role4(s, k):
        if k in by_z:
            at = spot(s, k, across, q_y, quarter)
            return push(s, k, 4, at, at, me, znbr)
        at = spot(s, k, across, q_z, quarter)
        return push(s, k, 4, at, at, me, ynbr)

    def two_steps(s, k):
        return s == 0 or DIRECT[k] == 0

    def role5(s, k):
        at = spot(s, k, across, 0, depth)
        return push(s, k, 5, at, at, sib, mine)

    def arrived(s, k, role):
        if role == 0:
            at = spot(s, k, across, *direct_rows(s, k))
        elif role == 1:
            at = spot(s, k, sib, 0, depth)
        elif role == 2:
            at = spot(s, k, across, *relay_rows(s, k, False))
        elif role == 3:
            at = spot(s, k, across, q_z, quarter)
        elif role == 4:
            at = spot(s, k, across, q_d, quarter)
        else:
            at = spot(s, k, (sib + 2) % nt_, 0, depth)
        push(s, k, role, at, at, sib, mine).wait_recv()

    turns = (mine // (ng // 2), 1 - mine // (ng // 2))

    def tr_copy(n, d):
        t = (me + d) % nt_
        src, dst = tr_ends(n, t, me)
        return remote(src, dst, tr_send.at[n, d], tr_recv.at[n, d], t, mine)

    def tr_ends(n, to, source):
        if n == 0:
            return tok.at[:, to], tokr.at[:, :, :, source]
        h, j = (n - 1) // 2, turns[(n - 1) % 2]
        pair = pl.ds(2 * j, 2)
        return outs.at[h, :, pair, to], out.at[:, source, h, pair]

    def gz_ends(n, to, source):
        if n < 2:
            h = n
            return mids.at[h, :, to // 2, :, to % 2], midr.at[h, pl.ds(source * slab, slab)]
        h = n - 2
        return grads.at[h, pl.ds(to * slab, slab)], gradr.at[h, :, source // 2, :, source % 2]

    def gz_copy(n, d):
        g = (mine + d) % ng
        src, dst = gz_ends(n, g, mine)
        return remote(src, dst, gz_send.at[n, d], gz_recv.at[n, d], me, g)

    far_first = [2, 3, 1] if nt_ == 4 else list(range(1, nt_))
    gz_order = sorted(range(1, ng), key=lambda d: -min(d, ng - d))

    def tr_begin(n):
        for d in far_first:
            tr_copy(n, d).start()

    def tr_end(n):
        for d in range(1, nt_):
            tr_copy(n, d).wait_send()
            src = (me + nt_ - d) % nt_
            at = tr_ends(n, me, src)[1]
            remote(at, at, tr_send.at[n, d], tr_recv.at[n, d], src, mine).wait_recv()

    def gz_begin(n):
        for d in gz_order:
            gz_copy(n, d).start()

    def gz_end(n):
        for d in range(1, ng):
            gz_copy(n, d).wait_send()
            src = (mine + ng - d) % ng
            at = gz_ends(n, mine, src)[1]
            remote(at, at, gz_send.at[n, d], gz_recv.at[n, d], me, src).wait_recv()

    core, zc, zs = me % 2, mine // 2, ng // 2
    lanes = (me, sib, across, (sib + 2) % nt_)

    def halves(j):
        return (0,) if j < 2 else range(parts)

    def cot_ends(j, to, z, source, at_x, h):
        if j < 2:
            return cot.at[:, to, :, z], cotz.at[pl.ds(source * slab, slab), :, at_x]
        return cot.at[:, to, h, z], cotz.at[pl.ds(source * slab, slab), h, at_x]

    def cot_copy(j, dz, h):
        z = (zc + dz) % zs
        src, dst = cot_ends(j, lanes[j], z, mine, me // 2, h)
        return remote(src, dst, c_send.at[j, dz, h], c_recv.at[j, dz, gy, h], lanes[j], 2 * z + core)

    def unless_self(j, dz, act):
        if j == 0 and dz == 0:
            pl.when(core != gy)(act)
        else:
            act()

    def cot_begin(js, h=0):
        for dz in (2, 1, 3, 0):
            for j in js:
                unless_self(j, dz, lambda: cot_copy(j, dz, h).start())

    def cot_end(h):
        other = (core + gy) % 2
        for i in range(2):
            if i == 0 and h > 0:
                continue
            at_x = (me // 2 + i) % 2
            for dz in range(zs):
                for ys in range(2):
                    g = 2 * ((zc + zs - dz) % zs) + ys
                    at = cot_ends(2 * i, me, zc, g, at_x, h)[1]
                    copy = remote(at, at, c_send.at[0, 0, 0], c_recv.at[other + 2 * i, dz, ys, h], sib, mine)
                    if i == 0 and dz == 0:
                        pl.when((core != gy) | (gy != ys))(lambda: copy.wait_recv())
                    else:
                        copy.wait_recv()
        if h == 0:
            pl.when(core == gy)(lambda: cot_self().wait())

    def cot_sent():
        for dz in range(zs):
            for j in range(4):
                for h in halves(j):
                    unless_self(j, dz, lambda: cot_copy(j, dz, h).wait_send())

    def cot_self():
        return pltpu.make_async_copy(cot.at[:, me, :, zc], cotz.at[pl.ds(mine * slab, slab), :, me // 2], local.at[7])

    ks = range(4)

    def begin_w1(pieces):
        for k in pieces:
            role0(1, k).start()

    for k in ks:
        role0(0, k).start()
    for k in ks:
        role1(0, k).start()
    pl.when(core == gy)(lambda: cot_self().start())
    for step in range(3):
        widen(step)
    if COT0 == 0:
        cot_begin((0,))
    if WIDE == 0:
        widen(3)
        cot_begin((1,))
    for k in ks:
        arrived(0, k, 0)
        role2(0, k).start()
        role3(0, k).start()
        if k == 0 and WIDE == 1:
            widen(3)
            if COT0 == 0:
                cot_begin((1,))
        if k == TOK_AFTER:
            tr_begin(0)
        begin_w1([j for j in ks if W1_AT[j] == k])
        if COT1 == k:
            cot_begin((2, 3))
    for k in ks:
        arrived(0, k, 2)
        if k in by_z:
            role4(0, k).start()
        arrived(0, k, 3)
        if k not in by_z:
            role4(0, k).start()
    if COT0 == 4:
        cot_begin((0, 1))
    begin_w1([j for j in ks if W1_AT[j] == 4])
    if COT1 == 4:
        cot_begin((2, 3))
        if COT2 < 0:
            cot_begin((2, 3), 1)
    for k in ks:
        arrived(0, k, 4)
        role5(0, k).start()
    for copy in here:
        copy.wait()
    tr_end(0)
    begin_w1([j for j in ks if W1_AT[j] == 5])
    if COT1 == 5:
        cot_begin((2, 3))
    for k in ks:
        role1(1, k).start()
    for h in range(parts):
        for j in range(2):
            ax[pl.ds(h * half + j * block, block)] = tokr[:, h, 2 * j : 2 * j + 2].reshape(block, width)
    for k in ks:
        arrived(0, k, 1)
        arrived(0, k, 5)

    def relay_z(pieces):
        for k in pieces:
            arrived(1, k, 0)
            role2(1, k).start()
            if over_z(1, k):
                role3(1, k).start()

    mask_x = line_mask(block, line_x, False)
    mask_z = line_mask(block, block // (slab * ng), True)
    gx, gz = gain_x[...][None], gain_z[...][None]
    for h in range(parts):
        at = pl.ds(h * half, half)
        a = ax[at].astype(F32)
        project(a, rms(a), gx, fwx, qkvx.at[at])
        attend_forward(qkvx.at[at], probs, 2 * h, mixed.at[at], mask_x)
        mid = ax[at].astype(F32) + nn(mixed[at], fox[...])
        mid = mid.astype(BF16)
        for j in range(2):
            spots = mids.at[h, :, 2 * j : 2 * j + 2]
            spots[...] = mid[j * block : (j + 1) * block].reshape(spots.shape)
        gz_begin(h)
        midr[h, pl.ds(mine * slab, slab)] = mids[h, :, mine // 2, :, mine % 2]
        if h == COT2:
            cot_begin((2, 3), 1)
        if h == 0:
            relay_z(RELAY1)
    def turn(pieces):
        for k in pieces:
            at = pl.ds((k % 3) * width, width)
            turned = (oxt if k == 3 else wxt).at[at]
            turned[...] = full_w[0][k][:, (k % 3) * width : (k % 3 + 1) * width].T

    turn(T0)
    relay_z([k for k in ks if k not in RELAY1])
    turn(T1)
    for k in ks:
        arrived(1, k, 2)
        if over_z(1, k):
            arrived(1, k, 3)
        if two_steps(1, k):
            role4(1, k).start()
        else:
            role5(1, k).start()
    for k in ks:
        if two_steps(1, k):
            arrived(1, k, 4)
            role5(1, k).start()
    for k in ks:
        arrived(1, k, 1)
        arrived(1, k, 5)

    def z_front(h):
        at = pl.ds(h * half, half)
        gz_end(h)
        for j in range(2):
            az[pl.ds(h * half + j * block, block)] = midr[h, :, j].reshape(block, width)
        a = az[at].astype(F32)
        rstd = rms(a)
        project(a, rstd, gz, fwz, qkvz.at[at])
        attend_scores(qkvz.at[at], probz, 2 * h, mask_z)
        return rstd

    for h in range(parts):
        at = pl.ds(h * half, half)
        rstd = z_front(h)
        cot_end(h)
        for j in range(2):
            cz[pl.ds(h * half + j * block, block)] = cotz[:, h, j].reshape(block, width)
        dmix[at] = nt(cz[at], foz[...]).astype(BF16)
        attend_backward(qkvz.at[at], probz, 2 * h, dmix.at[at], joined.at[at])
        back = norm_backward(
            az[at].astype(F32), cz[at].astype(F32), rstd, gz, joined.at[at], fwz, dn.at[at], False
        )
        for j in range(2):
            grads[h, :, j] = back[j * block : (j + 1) * block].reshape(slab * ng, block // (slab * ng), width)
        gz_begin(2 + h)
        gradr[h, :, mine // 2, :, mine % 2] = grads[h, pl.ds(mine * slab, slab)]

    def grads_here(n, j, near):
        count = ng // 2
        for d in range(1 if near else 0, count):
            g = j * count + ((mine + d) % count if near else d)
            at = gz_ends(n, mine, g)[1]
            remote(at, at, gz_send.at[n, 0], gz_recv.at[n, (mine + ng - g) % ng], me, g).wait_recv()

    turn(T2)
    kept = []
    for h in range(parts):
        for i, j in enumerate(turns):
            at = pl.ds(pl.multiple_of(h * half + j * block, 16), block)
            pair = pl.ds(2 * j, 2)
            a = ax[at].astype(F32)
            rstd = rms(a)
            grads_here(2 + h, j, i == 0)
            c = gradr[h, :, pair].reshape(block, width)
            dmix[at] = nn(c, oxt[...]).astype(BF16)
            attend_backward(qkvx.at[at], probs, 2 * h + j, dmix.at[at], joined.at[at])
            back = norm_backward(
                ax[at].astype(F32), c.astype(F32), rstd, gx, joined.at[at], wxt, dn.at[at], True
            )
            spots = outs.at[h, :, pair]
            spots[...] = back.reshape(spots.shape)
            n = 1 + 2 * h + i
            tr_begin(n)
            keep = pltpu.make_async_copy(*tr_ends(n, me, me), local.at[7 + n])
            keep.start()
            kept.append(keep)

    for k in ks:
        for s in range(2):
            role0(s, k).wait_send()
            role1(s, k).wait_send()
            role2(s, k).wait_send()
            role5(s, k).wait_send()
            if over_z(s, k):
                role3(s, k).wait_send()
            if two_steps(s, k):
                role4(s, k).wait_send()
    cot_sent()
    for h in range(parts):
        for d in range(1, ng):
            gz_copy(2 + h, d).wait_send()
    for n, keep in enumerate(kept):
        tr_end(1 + n)
        keep.wait()


DIRECT = (1, 1, 1, 1)
TOK_AFTER = 0
W1_AT = (3, 3, 3, 3)
COT0, COT1 = 0, 4
NEAR, WIDE = False, 0
RELAY1 = (0, 1, 2, 3)
COT2 = -1
T0, T1 = (0, 1), (2, 3)
T2 = ()
VM = 56


def settle(given, out, held, came, went):
    count = given.shape[0]
    ins = [pltpu.make_async_copy(given.at[i], held.at[i], came.at[i]) for i in range(count)]
    outs = [pltpu.make_async_copy(held.at[i], out.at[i], went.at[i]) for i in range(count)]
    for copy in ins:
        copy.start()
    for a, b in zip(ins, outs):
        a.wait()
        b.start()
    for copy in outs:
        copy.wait()


def fits_kernel(trs, gzs, slab, y, x_own, width, depth):
    return (trs, gzs, y, x_own) == (4, 8, 32, 2) and (slab * trs * x_own * 4) % 32 == 0 and width % 128 == 0 and depth % 64 == 0


def fused(trs, gzs, tokens, cotangent, gain_x, wqkv_x, wo_x, gain_z, wqkv_z, wo_z):
    slab, y, x_own, width = tokens.shape
    x, z = x_own * trs, slab * gzs
    rows = slab * y * x_own
    parts, group = 2, gzs // 2
    split = (slab, trs, parts, group, x_own, width)
    block = rows // 4
    lines = (slab, group, 2, trs // 2, x_own, width)
    vm = pl.BlockSpec(memory_space=pltpu.VMEM)
    hbm = pl.BlockSpec(memory_space=pl.ANY)
    wide = wqkv_x.shape[1]
    result = pl.pallas_call(
        functools.partial(kernel, trs, gzs, x),
        out_shape=jax.ShapeDtypeStruct(split, BF16),
        in_specs=[hbm, hbm, vm, hbm, hbm, vm, hbm, hbm],
        out_specs=hbm,
        scratch_shapes=[
            pltpu.VMEM((slab, parts, group, trs, x_own, width), BF16),
            pltpu.VMEM((z, parts, 2, x_own, width), BF16),
            pltpu.VMEM((parts, *lines), BF16),
            pltpu.VMEM((parts, z, 2, x_own, width), BF16),
            pltpu.VMEM((parts, z, 2, x_own, width), BF16),
            pltpu.VMEM((parts, *lines), BF16),
            pltpu.VMEM((parts, slab, group, trs, x_own, width), BF16),
        ]
        + [pltpu.VMEM((width, wide), BF16), pltpu.VMEM((width, width), BF16)] * 2
        + [pltpu.VMEM((wide, width), BF16), pltpu.VMEM((width, width), BF16)]
        + [pltpu.VMEM((rows, wide), BF16)] * 2
        + [pltpu.VMEM((4 * H, block, block), F32)] * 2
        + [pltpu.VMEM((rows, width), BF16)] * 2
        + [pltpu.VMEM((rows, wide), BF16), pltpu.VMEM((rows, width), F32)]
        + [pltpu.VMEM((rows, width), BF16)] * 3
        + [
            pltpu.SemaphoreType.DMA((5, trs)),
            pltpu.SemaphoreType.DMA((5, trs)),
            pltpu.SemaphoreType.DMA((4, gzs)),
            pltpu.SemaphoreType.DMA((4, gzs)),
            pltpu.SemaphoreType.DMA((2, 4, 6)),
            pltpu.SemaphoreType.DMA((2, 4, 6)),
            pltpu.SemaphoreType.DMA((4, gzs // 2, 2)),
            pltpu.SemaphoreType.DMA((4, gzs // 2, 2, 2)),
            pltpu.SemaphoreType.REGULAR((4,)),
            pltpu.SemaphoreType.DMA((12,)),
        ],
        compiler_params=pltpu.CompilerParams(
            collective_id=0, has_side_effects=True, vmem_limit_bytes=VM * 1024 * 1024
        ),
    )(
        tokens.reshape(split), cotangent.reshape(split),
        gain_x, wqkv_x, wo_x, gain_z, wqkv_z, wo_z,
    )
    return pl.pallas_call(
        settle,
        out_shape=jax.ShapeDtypeStruct(tokens.shape, BF16),
        in_specs=[hbm],
        out_specs=hbm,
        scratch_shapes=[
            pltpu.VMEM(tokens.shape, BF16),
            pltpu.SemaphoreType.DMA((slab,)),
            pltpu.SemaphoreType.DMA((slab,)),
        ],
    )(result.reshape(tokens.shape))


def solution(mesh):
    trs, gzs = mesh.shape["tr"], mesh.shape["gz"]

    def body(tokens, *rest):
        if fits_kernel(trs, gzs, *tokens.shape, rest[2].shape[0]):
            return fused(trs, gzs, tokens, *rest)
        return per_device(tokens, *rest)

    return jax.shard_map(
        body,
        mesh=mesh,
        in_specs=(
            P("gz", None, "tr", None),
            P("gz", None, "tr", None),
            P(),
            P("tr", None),
            P("tr", None),
            P(),
            P("tr", None),
            P("tr", None),
        ),
        out_specs=P("gz", None, "tr", None),
        check_vma=False,
    )
```

```python
import functools
import math

import jax
import jax.numpy as jnp
import numpy as np
from jax import lax
from jax.experimental import pallas as pl
from jax.experimental.pallas import tpu as pltpu
from jax.sharding import PartitionSpec as P

H = 6


def head_split(packed, index, model_width):
    piece = packed[..., index * model_width : (index + 1) * model_width]
    return piece.reshape(piece.shape[:-1] + (H, model_width // H))


def merge_heads(value):
    return value.reshape(value.shape[:-2] + (value.shape[-2] * value.shape[-1],))


def recompute(tokens_in, gain_vec, w_in, layout):
    model_width = w_in.shape[0]
    factor = 1.0 / math.sqrt(model_width // H)
    widened = tokens_in.astype(jnp.float32)
    inv_rms = lax.rsqrt(jnp.mean(widened * widened, axis=-1, keepdims=True) + 1e-06)
    normed = (widened * inv_rms * gain_vec).astype(jnp.bfloat16)
    packed = jnp.dot(normed, w_in, preferred_element_type=jnp.float32).astype(jnp.bfloat16)
    queries = head_split(packed, 0, model_width)
    key_part = head_split(packed, 1, model_width)
    values = head_split(packed, 2, model_width)
    key_form = layout.replace("l", "m")
    scores = (
        jnp.einsum(
            layout + "," + key_form + "->bhlm",
            queries,
            key_part,
            preferred_element_type=jnp.float32,
        )
        * factor
    )
    highest = jnp.max(scores, axis=-1, keepdims=True)
    expanded = jnp.exp(scores - highest)
    probs = expanded / jnp.sum(expanded, axis=-1, keepdims=True)
    return (widened, inv_rms, queries, key_part, values, probs, probs.astype(jnp.bfloat16), factor)


def forward_out(tokens_in, gain_vec, w_in, w_out, layout):
    widened, inv_rms, queries, key_part, values, probs, probs_b, factor = recompute(
        tokens_in, gain_vec, w_in, layout
    )
    key_form = layout.replace("l", "m")
    mixed = jnp.einsum(
        "bhlm," + key_form + "->" + layout, probs_b, values, preferred_element_type=jnp.float32
    )
    mixed = merge_heads(mixed.astype(jnp.bfloat16))
    return (widened + jnp.dot(mixed, w_out, preferred_element_type=jnp.float32)).astype(
        jnp.bfloat16
    )


def backward(tokens_in, upstream, gain_vec, w_in, w_out, layout):
    widened, inv_rms, queries, key_part, values, probs, probs_b, factor = recompute(
        tokens_in, gain_vec, w_in, layout
    )
    key_form = layout.replace("l", "m")
    d_mixed = jnp.dot(upstream, w_out.T, preferred_element_type=jnp.float32).astype(jnp.bfloat16)
    d_mixed = d_mixed.reshape(d_mixed.shape[:-1] + (H, d_mixed.shape[-1] // H))
    d_probs = jnp.einsum(
        layout + "," + key_form + "->bhlm", d_mixed, values, preferred_element_type=jnp.float32
    )
    d_values = jnp.einsum(
        "bhlm," + layout + "->" + key_form, probs_b, d_mixed, preferred_element_type=jnp.float32
    ).astype(jnp.bfloat16)
    centre = jnp.sum(probs * d_probs, axis=-1, keepdims=True)
    d_scores = (probs * (d_probs - centre) * factor).astype(jnp.bfloat16)
    d_queries = jnp.einsum(
        "bhlm," + key_form + "->" + layout, d_scores, key_part, preferred_element_type=jnp.float32
    ).astype(jnp.bfloat16)
    d_keys = jnp.einsum(
        "bhlm," + layout + "->" + key_form, d_scores, queries, preferred_element_type=jnp.float32
    ).astype(jnp.bfloat16)
    joined = jnp.concatenate(
        [merge_heads(d_queries), merge_heads(d_keys), merge_heads(d_values)], axis=-1
    )
    d_normed = jnp.dot(joined, w_in.T, preferred_element_type=jnp.float32)
    scaled = d_normed * gain_vec
    d_tokens = inv_rms * (
        scaled - widened * inv_rms * inv_rms * jnp.mean(scaled * widened, axis=-1, keepdims=True)
    )
    return (upstream.astype(jnp.float32) + d_tokens).astype(jnp.bfloat16)


def line_forward(lines, gain_vec, w_in, w_out):
    feature_count = lines.shape[3]
    flat = lines.reshape(-1, lines.shape[2], feature_count)
    return forward_out(flat, gain_vec, w_in, w_out, "blhe").reshape(lines.shape)


def line_backward(lines, upstream, gain_vec, w_in, w_out):
    feature_count = lines.shape[3]
    flat = lines.reshape(-1, lines.shape[2], feature_count)
    flat_up = upstream.reshape(flat.shape)
    return backward(flat, flat_up, gain_vec, w_in, w_out, "blhe").reshape(lines.shape)


def per_device(tokens, cotangent, gain_x, wqkv_x, wo_x, gain_z, wqkv_z, wo_z):
    full_in_x, full_out_x = (
        lax.all_gather(wqkv_x, "tr", axis=0, tiled=True),
        lax.all_gather(wo_x, "tr", axis=0, tiled=True),
    )
    full_in_z, full_out_z = (
        lax.all_gather(wqkv_z, "tr", axis=0, tiled=True),
        lax.all_gather(wo_z, "tr", axis=0, tiled=True),
    )
    width = tokens.shape[-1]
    lines = lax.all_to_all(tokens, "tr", split_axis=1, concat_axis=2, tiled=True)
    cot_lines = lax.all_to_all(cotangent, "tr", split_axis=1, concat_axis=2, tiled=True)
    cells = lines.shape[1] * lines.shape[2]
    flat = (lines.shape[0], cells, width)
    cot_columns = lax.all_to_all(
        cot_lines.reshape(flat), "gz", split_axis=1, concat_axis=0, tiled=True
    )
    mid_lines = line_forward(lines, gain_x, full_in_x, full_out_x)
    mid_columns = lax.all_to_all(
        mid_lines.reshape(flat), "gz", split_axis=1, concat_axis=0, tiled=True
    )
    grad_columns = backward(
        mid_columns, cot_columns, gain_z, full_in_z, full_out_z, "lbhe"
    )
    grad_lines = lax.all_to_all(grad_columns, "gz", split_axis=0, concat_axis=1, tiled=True)
    result_lines = line_backward(lines, grad_lines.reshape(lines.shape), gain_x, full_in_x, full_out_x)
    return lax.all_to_all(result_lines, "tr", split_axis=2, concat_axis=1, tiled=True)


F32, BF16 = jnp.float32, jnp.bfloat16


def nt(a, b):
    return lax.dot_general(a, b, (((1,), (1,)), ((), ())), preferred_element_type=F32)


def tn(a, b):
    return lax.dot_general(a, b, (((0,), (0,)), ((), ())), preferred_element_type=F32)


def nn(a, b):
    return jnp.dot(a, b, preferred_element_type=F32)


def rms(a):
    return lax.rsqrt(jnp.mean(a * a, axis=-1, keepdims=True) + 1e-06)


def project(a, rstd, gain, w, qkv):
    width = a.shape[1]
    normed = (a * rstd * gain).astype(BF16)
    for j in range(3):
        cols = slice(j * width, (j + 1) * width)
        qkv[:, cols] = nn(normed, w[:, cols]).astype(BF16)


def line_mask(block, line, inner):
    key = lax.broadcasted_iota(jnp.int32, (block, block), 0)
    query = lax.broadcasted_iota(jnp.int32, (block, block), 1)
    if inner:
        return key % line == query % line
    return key // line == query // line


def head_spans(width):
    size = width // H
    return [[pl.ds(n * width + h * size, size) for n in range(3)] for h in range(H)]


def softmax_rows(qkv, at, spans, mask, factor):
    qk = [nt(qkv[at, sp[1]], qkv[at, sp[0]]) for sp in spans]
    scores = [jnp.where(mask, x * factor, -1e30) for x in qk]
    tops = [jnp.max(x, axis=0, keepdims=True) for x in scores]
    grown = [jnp.exp(x - t) for x, t in zip(scores, tops)]
    sums = [1.0 / jnp.sum(x, axis=0, keepdims=True) for x in grown]
    return [x * t for x, t in zip(grown, sums)]


def attend_scores(qkv, probs, first, mask):
    rows = qkv.shape[0]
    width = qkv.shape[1] // 3
    block = mask.shape[0]
    factor = 1.0 / math.sqrt(width // H)
    for b in range(rows // block):
        ps = softmax_rows(qkv, pl.ds(b * block, block), head_spans(width), mask, factor)
        for h, p in enumerate(ps):
            probs[(first + b) * H + h] = p


def attend_forward(qkv, probs, first, mixed, mask):
    rows, width = mixed.shape
    block = mask.shape[0]
    factor = 1.0 / math.sqrt(width // H)
    spans = head_spans(width)
    for b in range(rows // block):
        at = pl.ds(b * block, block)
        ps = softmax_rows(qkv, at, spans, mask, factor)
        for h, p in enumerate(ps):
            probs[(first + b) * H + h] = p
        outs = [tn(p.astype(BF16), qkv[at, sp[2]]) for p, sp in zip(ps, spans)]
        for sp, o in zip(spans, outs):
            mixed[at, sp[0]] = o.astype(BF16)


def attend_backward(qkv, probs, first, d_mixed, joined):
    rows, width = d_mixed.shape
    block = probs.shape[1]
    factor = 1.0 / math.sqrt(width // H)
    spans = head_spans(width)
    for b in range(rows // block):
        at = pl.ds(b * block, block)
        dps = [nt(qkv[at, sp[2]], d_mixed[at, sp[0]]) for sp in spans]
        ps = [probs[(first + b) * H + h] for h in range(H)]
        dvs = [nn(p.astype(BF16), d_mixed[at, sp[0]]) for p, sp in zip(ps, spans)]
        centres = [jnp.sum(p * dp, axis=0, keepdims=True) for p, dp in zip(ps, dps)]
        dss = [(p * (dp - c) * factor).astype(BF16) for p, dp, c in zip(ps, dps, centres)]
        dks = [nn(ds, qkv[at, sp[0]]) for ds, sp in zip(dss, spans)]
        dqs = [tn(ds, qkv[at, sp[1]]) for ds, sp in zip(dss, spans)]
        for sp, dq, dk, dv in zip(spans, dqs, dks, dvs):
            joined[at, sp[0]] = dq.astype(BF16)
            joined[at, sp[1]] = dk.astype(BF16)
            joined[at, sp[2]] = dv.astype(BF16)


def norm_backward(a, c, rstd, gain, joined, w, dn, turned):
    width = a.shape[-1]
    part = width // 3
    for j in range(3):
        cols = slice(j * part, (j + 1) * part)
        dn[:, cols] = nn(joined[...], w[:, cols]) if turned else nt(joined[...], w[cols, :])
    scaled = dn[...] * gain
    mean = jnp.mean(scaled * a, axis=-1, keepdims=True)
    return (c + rstd * (scaled - a * (rstd * rstd) * mean)).astype(BF16)


def kernel(
    nt_, ng, line_x,
    tok, cot, gain_x, wx, ox, gain_z, wz, oz, out,
    tokr, cotz, mids, midr, grads, gradr, outs,
    fwx, fox, fwz, foz, wxt, oxt, qkvx, qkvz, probs, probz, mixed, dmix, joined, dn, ax, az, cz,
    tr_send, tr_recv, gz_send, gz_recv, w_send, w_recv, c_send, c_recv, entered, local,
):
    me, mine = lax.axis_index("tr"), lax.axis_index("gz")
    sib, across = me + 1 - 2 * (me % 2), (me + 2) % nt_
    gy, gp = mine % 2, (mine // 2) % 2
    ynbr, znbr = mine + 1 - 2 * gy, mine + 2 - 4 * gp
    slab, pairs, width = tok.shape[0], tok.shape[3], tok.shape[5]
    parts = tok.shape[2]
    half = ax.shape[0] // parts
    block = half // 2

    def tell(sem, t, g):
        pl.semaphore_signal(sem, inc=1, device_id=(t, g), device_id_type=pl.DeviceIdType.MESH)

    zrow, last = mine // 2, ng // 2 - 1

    def tell_lanes(sem):
        for d in range(1, nt_):
            tell(sem, (me + d) % nt_, mine)

    def tell_near(sem):
        tell(sem, me, ynbr)
        pl.when(zrow > 0)(lambda: tell(sem, me, mine - 2))
        pl.when(zrow < last)(lambda: tell(sem, me, mine + 2))

    near = 1 + (zrow + last) // (last + 1) + (2 * last - zrow) // (last + 1)

    barrier = pltpu.get_barrier_semaphore()
    tell_lanes(barrier)
    if NEAR:
        tell_near(barrier)
    else:
        for d in range(1, ng):
            tell(barrier, me, (mine + d) % ng)

    own_w = ((wx, wx, wx, ox), (wz, wz, wz, oz))
    full_w = ((fwx, fwx, fwx, fox), (fwz, fwz, fwz, foz))
    depth = wx.shape[0]
    quarter = depth // 4

    here = [
        pltpu.make_async_copy(tok.at[:, me], tokr.at[:, :, :, me], local.at[0]),
    ]
    for s in range(2):
        for k in (0, 3):
            to = full_w[s][k].at[pl.ds(pl.multiple_of(me * depth, 16), depth)]
            here.append(pltpu.make_async_copy(own_w[s][k], to, local.at[len(here)]))
    for copy in here:
        copy.start()

    if NEAR:
        pl.semaphore_wait(barrier, nt_ - 1 + near)
        tell_near(entered.at[0])
    else:
        pl.semaphore_wait(barrier, nt_ + ng - 2)
        tell_lanes(entered.at[3])

    def widen(step):
        if step < 3:
            if NEAR:
                pl.semaphore_wait(entered.at[step], near)
                if step < 2:
                    tell_near(entered.at[step + 1])
                else:
                    tell_lanes(entered.at[3])
        else:
            pl.semaphore_wait(entered.at[3], nt_ - 1)

    def remote(src, dst, send, recv, t, g):
        return pltpu.make_async_remote_copy(
            src_ref=src, dst_ref=dst, send_sem=send, recv_sem=recv,
            device_id=(t, g), device_id_type=pl.DeviceIdType.MESH,
        )

    def own(s, k, row, n):
        at = pl.ds(pl.multiple_of(row, 16), n)
        return own_w[s][k].at[at, pl.ds((k % 3) * width, width)]

    def spot(s, k, shard, row, n):
        at = pl.ds(pl.multiple_of(shard * depth + row, 16), n)
        return full_w[s][k].at[at, pl.ds((k % 3) * width, width)]

    def push(s, k, role, src, dst, t, g):
        return remote(src, dst, w_send.at[s, k, role], w_recv.at[s, k, role], t, g)

    odd = (gy + gp) % 2
    q_me, q_d = (2 * odd + gy) * quarter, (2 * odd + 1 - gy) * quarter
    q_y, q_z = (3 - 2 * odd - gy) * quarter, (2 - 2 * odd + gy) * quarter
    by_z = (0, 1)

    def direct_rows(s, k):
        if s == 0 or DIRECT[k] == 0:
            return q_me, quarter
        if DIRECT[k] == 1:
            return 2 * odd * quarter, 2 * quarter
        n = DIRECT[k] * quarter
        return gy * (depth - n), n

    def relay_rows(s, k, sent):
        if s == 0 or DIRECT[k] <= 1:
            return (q_me if sent else q_y), quarter
        n = DIRECT[k] * quarter
        return (gy if sent else 1 - gy) * n, depth - n

    def over_z(s, k):
        return s == 0 or DIRECT[k] <= 1

    def role0(s, k):
        row, n = direct_rows(s, k)
        return push(s, k, 0, own(s, k, row, n), spot(s, k, me, row, n), across, mine)

    def role1(s, k):
        return push(s, k, 1, own(s, k, 0, depth), spot(s, k, me, 0, depth), sib, mine)

    def role2(s, k):
        row, n = relay_rows(s, k, True)
        at = spot(s, k, across, row, n)
        return push(s, k, 2, at, at, me, ynbr)

    def role3(s, k):
        at = spot(s, k, across, q_me, quarter)
        return push(s, k, 3, at, at, me, znbr)

    def role4(s, k):
        if k in by_z:
            at = spot(s, k, across, q_y, quarter)
            return push(s, k, 4, at, at, me, znbr)
        at = spot(s, k, across, q_z, quarter)
        return push(s, k, 4, at, at, me, ynbr)

    def two_steps(s, k):
        return s == 0 or DIRECT[k] == 0

    def role5(s, k):
        at = spot(s, k, across, 0, depth)
        return push(s, k, 5, at, at, sib, mine)

    def arrived(s, k, role):
        if role == 0:
            at = spot(s, k, across, *direct_rows(s, k))
        elif role == 1:
            at = spot(s, k, sib, 0, depth)
        elif role == 2:
            at = spot(s, k, across, *relay_rows(s, k, False))
        elif role == 3:
            at = spot(s, k, across, q_z, quarter)
        elif role == 4:
            at = spot(s, k, across, q_d, quarter)
        else:
            at = spot(s, k, (sib + 2) % nt_, 0, depth)
        push(s, k, role, at, at, sib, mine).wait_recv()

    turns = (mine // (ng // 2), 1 - mine // (ng // 2))

    def tr_copy(n, d):
        t = (me + d) % nt_
        src, dst = tr_ends(n, t, me)
        return remote(src, dst, tr_send.at[n, d], tr_recv.at[n, d], t, mine)

    def tr_ends(n, to, source):
        if n == 0:
            return tok.at[:, to], tokr.at[:, :, :, source]
        h, j = (n - 1) // 2, turns[(n - 1) % 2]
        pair = pl.ds(2 * j, 2)
        return outs.at[h, :, pair, to], out.at[:, source, h, pair]

    def gz_ends(n, to, source):
        if n < 2:
            h = n
            return mids.at[h, :, to // 2, :, to % 2], midr.at[h, pl.ds(source * slab, slab)]
        h = n - 2
        return grads.at[h, pl.ds(to * slab, slab)], gradr.at[h, :, source // 2, :, source % 2]

    def gz_copy(n, d):
        g = (mine + d) % ng
        src, dst = gz_ends(n, g, mine)
        return remote(src, dst, gz_send.at[n, d], gz_recv.at[n, d], me, g)

    far_first = [2, 3, 1] if nt_ == 4 else list(range(1, nt_))
    gz_order = sorted(range(1, ng), key=lambda d: -min(d, ng - d))

    def tr_begin(n):
        for d in far_first:
            tr_copy(n, d).start()

    def tr_end(n):
        for d in range(1, nt_):
            tr_copy(n, d).wait_send()
            src = (me + nt_ - d) % nt_
            at = tr_ends(n, me, src)[1]
            remote(at, at, tr_send.at[n, d], tr_recv.at[n, d], src, mine).wait_recv()

    def gz_begin(n):
        for d in gz_order:
            gz_copy(n, d).start()

    def gz_end(n):
        for d in range(1, ng):
            gz_copy(n, d).wait_send()
            src = (mine + ng - d) % ng
            at = gz_ends(n, mine, src)[1]
            remote(at, at, gz_send.at[n, d], gz_recv.at[n, d], me, src).wait_recv()

    core, zc, zs = me % 2, mine // 2, ng // 2
    lanes = (me, sib, across, (sib + 2) % nt_)

    def halves(j):
        return (0,) if j < 2 else range(parts)

    def cot_ends(j, to, z, source, at_x, h):
        if j < 2:
            return cot.at[:, to, :, z], cotz.at[pl.ds(source * slab, slab), :, at_x]
        return cot.at[:, to, h, z], cotz.at[pl.ds(source * slab, slab), h, at_x]

    def cot_copy(j, dz, h):
        z = (zc + dz) % zs
        src, dst = cot_ends(j, lanes[j], z, mine, me // 2, h)
        return remote(src, dst, c_send.at[j, dz, h], c_recv.at[j, dz, gy, h], lanes[j], 2 * z + core)

    def unless_self(j, dz, act):
        if j == 0 and dz == 0:
            pl.when(core != gy)(act)
        else:
            act()

    def cot_begin(js, h=0):
        for dz in (2, 1, 3, 0):
            for j in js:
                unless_self(j, dz, lambda: cot_copy(j, dz, h).start())

    def cot_end(h):
        other = (core + gy) % 2
        for i in range(2):
            if i == 0 and h > 0:
                continue
            at_x = (me // 2 + i) % 2
            for dz in range(zs):
                for ys in range(2):
                    g = 2 * ((zc + zs - dz) % zs) + ys
                    at = cot_ends(2 * i, me, zc, g, at_x, h)[1]
                    copy = remote(at, at, c_send.at[0, 0, 0], c_recv.at[other + 2 * i, dz, ys, h], sib, mine)
                    if i == 0 and dz == 0:
                        pl.when((core != gy) | (gy != ys))(lambda: copy.wait_recv())
                    else:
                        copy.wait_recv()
        if h == 0:
            pl.when(core == gy)(lambda: cot_self().wait())

    def cot_sent():
        for dz in range(zs):
            for j in range(4):
                for h in halves(j):
                    unless_self(j, dz, lambda: cot_copy(j, dz, h).wait_send())

    def cot_self():
        return pltpu.make_async_copy(cot.at[:, me, :, zc], cotz.at[pl.ds(mine * slab, slab), :, me // 2], local.at[7])

    ks = range(4)

    def begin_w1(pieces):
        for k in pieces:
            role0(1, k).start()

    for k in ks:
        role0(0, k).start()
    for k in ks:
        role1(0, k).start()
    pl.when(core == gy)(lambda: cot_self().start())
    for step in range(3):
        widen(step)
    if COT0 == 0:
        cot_begin((0,))
    if WIDE == 0:
        widen(3)
        cot_begin((1,))
    for k in ks:
        arrived(0, k, 0)
        role2(0, k).start()
        role3(0, k).start()
        if k == 0 and WIDE == 1:
            widen(3)
            if COT0 == 0:
                cot_begin((1,))
        if k == TOK_AFTER:
            tr_begin(0)
        begin_w1([j for j in ks if W1_AT[j] == k])
        if COT1 == k:
            cot_begin((2, 3))
    for k in ks:
        arrived(0, k, 2)
        if k in by_z:
            role4(0, k).start()
        arrived(0, k, 3)
        if k not in by_z:
            role4(0, k).start()
    if COT0 == 4:
        cot_begin((0, 1))
    begin_w1([j for j in ks if W1_AT[j] == 4])
    if COT1 == 4:
        cot_begin((2, 3))
        if COT2 < 0:
            cot_begin((2, 3), 1)
    for k in ks:
        arrived(0, k, 4)
        role5(0, k).start()
    for copy in here:
        copy.wait()
    tr_end(0)
    begin_w1([j for j in ks if W1_AT[j] == 5])
    if COT1 == 5:
        cot_begin((2, 3))
    for k in ks:
        role1(1, k).start()
    for h in range(parts):
        for j in range(2):
            ax[pl.ds(h * half + j * block, block)] = tokr[:, h, 2 * j : 2 * j + 2].reshape(block, width)
    for k in ks:
        arrived(0, k, 1)
        arrived(0, k, 5)

    def relay_z(pieces):
        for k in pieces:
            arrived(1, k, 0)
            role2(1, k).start()
            if over_z(1, k):
                role3(1, k).start()

    mask_x = line_mask(block, line_x, False)
    mask_z = line_mask(block, block // (slab * ng), True)
    gx, gz = gain_x[...][None], gain_z[...][None]
    for h in range(parts):
        at = pl.ds(h * half, half)
        a = ax[at].astype(F32)
        project(a, rms(a), gx, fwx, qkvx.at[at])
        attend_forward(qkvx.at[at], probs, 2 * h, mixed.at[at], mask_x)
        mid = ax[at].astype(F32) + nn(mixed[at], fox[...])
        mid = mid.astype(BF16)
        for j in range(2):
            spots = mids.at[h, :, 2 * j : 2 * j + 2]
            spots[...] = mid[j * block : (j + 1) * block].reshape(spots.shape)
        gz_begin(h)
        midr[h, pl.ds(mine * slab, slab)] = mids[h, :, mine // 2, :, mine % 2]
        if h == COT2:
            cot_begin((2, 3), 1)
        if h == 0:
            relay_z(RELAY1)
    def turn(pieces):
        for k in pieces:
            at = pl.ds((k % 3) * width, width)
            turned = (oxt if k == 3 else wxt).at[at]
            turned[...] = full_w[0][k][:, (k % 3) * width : (k % 3 + 1) * width].T

    turn(T0)
    relay_z([k for k in ks if k not in RELAY1])
    turn(T1)
    for k in ks:
        arrived(1, k, 2)
        if over_z(1, k):
            arrived(1, k, 3)
        if two_steps(1, k):
            role4(1, k).start()
        else:
            role5(1, k).start()
    for k in ks:
        if two_steps(1, k):
            arrived(1, k, 4)
            role5(1, k).start()
    for k in ks:
        arrived(1, k, 1)
        arrived(1, k, 5)

    def z_front(h):
        at = pl.ds(h * half, half)
        gz_end(h)
        for j in range(2):
            az[pl.ds(h * half + j * block, block)] = midr[h, :, j].reshape(block, width)
        a = az[at].astype(F32)
        rstd = rms(a)
        project(a, rstd, gz, fwz, qkvz.at[at])
        attend_scores(qkvz.at[at], probz, 2 * h, mask_z)
        return rstd

    for h in range(parts):
        at = pl.ds(h * half, half)
        rstd = z_front(h)
        cot_end(h)
        for j in range(2):
            cz[pl.ds(h * half + j * block, block)] = cotz[:, h, j].reshape(block, width)
        dmix[at] = nt(cz[at], foz[...]).astype(BF16)
        attend_backward(qkvz.at[at], probz, 2 * h, dmix.at[at], joined.at[at])
        back = norm_backward(
            az[at].astype(F32), cz[at].astype(F32), rstd, gz, joined.at[at], fwz, dn.at[at], False
        )
        for j in range(2):
            grads[h, :, j] = back[j * block : (j + 1) * block].reshape(slab * ng, block // (slab * ng), width)
        gz_begin(2 + h)
        gradr[h, :, mine // 2, :, mine % 2] = grads[h, pl.ds(mine * slab, slab)]

    def grads_here(n, j, near):
        count = ng // 2
        for d in range(1 if near else 0, count):
            g = j * count + ((mine + d) % count if near else d)
            at = gz_ends(n, mine, g)[1]
            remote(at, at, gz_send.at[n, 0], gz_recv.at[n, (mine + ng - g) % ng], me, g).wait_recv()

    turn(T2)
    kept = []
    for h in range(parts):
        for i, j in enumerate(turns):
            at = pl.ds(pl.multiple_of(h * half + j * block, 16), block)
            pair = pl.ds(2 * j, 2)
            a = ax[at].astype(F32)
            rstd = rms(a)
            grads_here(2 + h, j, i == 0)
            c = gradr[h, :, pair].reshape(block, width)
            dmix[at] = nn(c, oxt[...]).astype(BF16)
            attend_backward(qkvx.at[at], probs, 2 * h + j, dmix.at[at], joined.at[at])
            back = norm_backward(
                ax[at].astype(F32), c.astype(F32), rstd, gx, joined.at[at], wxt, dn.at[at], True
            )
            spots = outs.at[h, :, pair]
            spots[...] = back.reshape(spots.shape)
            n = 1 + 2 * h + i
            tr_begin(n)
            keep = pltpu.make_async_copy(*tr_ends(n, me, me), local.at[7 + n])
            keep.start()
            kept.append(keep)

    for k in ks:
        for s in range(2):
            role0(s, k).wait_send()
            role1(s, k).wait_send()
            role2(s, k).wait_send()
            role5(s, k).wait_send()
            if over_z(s, k):
                role3(s, k).wait_send()
            if two_steps(s, k):
                role4(s, k).wait_send()
    cot_sent()
    for h in range(parts):
        for d in range(1, ng):
            gz_copy(2 + h, d).wait_send()
    for n, keep in enumerate(kept):
        tr_end(1 + n)
        keep.wait()


DIRECT = (1, 1, 1, 1)
TOK_AFTER = 0
W1_AT = (3, 3, 3, 3)
COT0, COT1 = 0, 5
NEAR, WIDE = False, 0
RELAY1 = (0, 1, 2, 3)
COT2 = 1
T0, T1 = (0, 1), (2, 3)
T2 = ()
VM = 56


def settle(given, out, held, came, went):
    count = given.shape[0]
    ins = [pltpu.make_async_copy(given.at[i], held.at[i], came.at[i]) for i in range(count)]
    outs = [pltpu.make_async_copy(held.at[i], out.at[i], went.at[i]) for i in range(count)]
    for copy in ins:
        copy.start()
    for a, b in zip(ins, outs):
        a.wait()
        b.start()
    for copy in outs:
        copy.wait()


def fits_kernel(trs, gzs, slab, y, x_own, width, depth):
    return (trs, gzs, y, x_own) == (4, 8, 32, 2) and (slab * trs * x_own * 4) % 32 == 0 and width % 128 == 0 and depth % 64 == 0


def fused(trs, gzs, tokens, cotangent, gain_x, wqkv_x, wo_x, gain_z, wqkv_z, wo_z):
    slab, y, x_own, width = tokens.shape
    x, z = x_own * trs, slab * gzs
    rows = slab * y * x_own
    parts, group = 2, gzs // 2
    split = (slab, trs, parts, group, x_own, width)
    block = rows // 4
    lines = (slab, group, 2, trs // 2, x_own, width)
    vm = pl.BlockSpec(memory_space=pltpu.VMEM)
    hbm = pl.BlockSpec(memory_space=pl.ANY)
    wide = wqkv_x.shape[1]
    result = pl.pallas_call(
        functools.partial(kernel, trs, gzs, x),
        out_shape=jax.ShapeDtypeStruct(split, BF16),
        in_specs=[hbm, hbm, vm, hbm, hbm, vm, hbm, hbm],
        out_specs=hbm,
        scratch_shapes=[
            pltpu.VMEM((slab, parts, group, trs, x_own, width), BF16),
            pltpu.VMEM((z, parts, 2, x_own, width), BF16),
            pltpu.VMEM((parts, *lines), BF16),
            pltpu.VMEM((parts, z, 2, x_own, width), BF16),
            pltpu.VMEM((parts, z, 2, x_own, width), BF16),
            pltpu.VMEM((parts, *lines), BF16),
            pltpu.VMEM((parts, slab, group, trs, x_own, width), BF16),
        ]
        + [pltpu.VMEM((width, wide), BF16), pltpu.VMEM((width, width), BF16)] * 2
        + [pltpu.VMEM((wide, width), BF16), pltpu.VMEM((width, width), BF16)]
        + [pltpu.VMEM((rows, wide), BF16)] * 2
        + [pltpu.VMEM((4 * H, block, block), F32)] * 2
        + [pltpu.VMEM((rows, width), BF16)] * 2
        + [pltpu.VMEM((rows, wide), BF16), pltpu.VMEM((rows, width), F32)]
        + [pltpu.VMEM((rows, width), BF16)] * 3
        + [
            pltpu.SemaphoreType.DMA((5, trs)),
            pltpu.SemaphoreType.DMA((5, trs)),
            pltpu.SemaphoreType.DMA((4, gzs)),
            pltpu.SemaphoreType.DMA((4, gzs)),
            pltpu.SemaphoreType.DMA((2, 4, 6)),
            pltpu.SemaphoreType.DMA((2, 4, 6)),
            pltpu.SemaphoreType.DMA((4, gzs // 2, 2)),
            pltpu.SemaphoreType.DMA((4, gzs // 2, 2, 2)),
            pltpu.SemaphoreType.REGULAR((4,)),
            pltpu.SemaphoreType.DMA((12,)),
        ],
        compiler_params=pltpu.CompilerParams(
            collective_id=0, has_side_effects=True, vmem_limit_bytes=VM * 1024 * 1024
        ),
    )(
        tokens.reshape(split), cotangent.reshape(split),
        gain_x, wqkv_x, wo_x, gain_z, wqkv_z, wo_z,
    )
    return pl.pallas_call(
        settle,
        out_shape=jax.ShapeDtypeStruct(tokens.shape, BF16),
        in_specs=[hbm],
        out_specs=hbm,
        scratch_shapes=[
            pltpu.VMEM(tokens.shape, BF16),
            pltpu.SemaphoreType.DMA((slab,)),
            pltpu.SemaphoreType.DMA((slab,)),
        ],
    )(result.reshape(tokens.shape))


def solution(mesh):
    trs, gzs = mesh.shape["tr"], mesh.shape["gz"]

    def body(tokens, *rest):
        if fits_kernel(trs, gzs, *tokens.shape, rest[2].shape[0]):
            return fused(trs, gzs, tokens, *rest)
        return per_device(tokens, *rest)

    return jax.shard_map(
        body,
        mesh=mesh,
        in_specs=(
            P("gz", None, "tr", None),
            P("gz", None, "tr", None),
            P(),
            P("tr", None),
            P("tr", None),
            P(),
            P("tr", None),
            P("tr", None),
        ),
        out_specs=P("gz", None, "tr", None),
        check_vma=False,
    )
```

```python
import functools
import math

import jax
import jax.numpy as jnp
import numpy as np
from jax import lax
from jax.experimental import pallas as pl
from jax.experimental.pallas import tpu as pltpu
from jax.sharding import PartitionSpec as P

H = 6


def head_split(packed, index, model_width):
    piece = packed[..., index * model_width : (index + 1) * model_width]
    return piece.reshape(piece.shape[:-1] + (H, model_width // H))


def merge_heads(value):
    return value.reshape(value.shape[:-2] + (value.shape[-2] * value.shape[-1],))


def recompute(tokens_in, gain_vec, w_in, layout):
    model_width = w_in.shape[0]
    factor = 1.0 / math.sqrt(model_width // H)
    widened = tokens_in.astype(jnp.float32)
    inv_rms = lax.rsqrt(jnp.mean(widened * widened, axis=-1, keepdims=True) + 1e-06)
    normed = (widened * inv_rms * gain_vec).astype(jnp.bfloat16)
    packed = jnp.dot(normed, w_in, preferred_element_type=jnp.float32).astype(jnp.bfloat16)
    queries = head_split(packed, 0, model_width)
    key_part = head_split(packed, 1, model_width)
    values = head_split(packed, 2, model_width)
    key_form = layout.replace("l", "m")
    scores = (
        jnp.einsum(
            layout + "," + key_form + "->bhlm",
            queries,
            key_part,
            preferred_element_type=jnp.float32,
        )
        * factor
    )
    highest = jnp.max(scores, axis=-1, keepdims=True)
    expanded = jnp.exp(scores - highest)
    probs = expanded / jnp.sum(expanded, axis=-1, keepdims=True)
    return (widened, inv_rms, queries, key_part, values, probs, probs.astype(jnp.bfloat16), factor)


def forward_out(tokens_in, gain_vec, w_in, w_out, layout):
    widened, inv_rms, queries, key_part, values, probs, probs_b, factor = recompute(
        tokens_in, gain_vec, w_in, layout
    )
    key_form = layout.replace("l", "m")
    mixed = jnp.einsum(
        "bhlm," + key_form + "->" + layout, probs_b, values, preferred_element_type=jnp.float32
    )
    mixed = merge_heads(mixed.astype(jnp.bfloat16))
    return (widened + jnp.dot(mixed, w_out, preferred_element_type=jnp.float32)).astype(
        jnp.bfloat16
    )


def backward(tokens_in, upstream, gain_vec, w_in, w_out, layout):
    widened, inv_rms, queries, key_part, values, probs, probs_b, factor = recompute(
        tokens_in, gain_vec, w_in, layout
    )
    key_form = layout.replace("l", "m")
    d_mixed = jnp.dot(upstream, w_out.T, preferred_element_type=jnp.float32).astype(jnp.bfloat16)
    d_mixed = d_mixed.reshape(d_mixed.shape[:-1] + (H, d_mixed.shape[-1] // H))
    d_probs = jnp.einsum(
        layout + "," + key_form + "->bhlm", d_mixed, values, preferred_element_type=jnp.float32
    )
    d_values = jnp.einsum(
        "bhlm," + layout + "->" + key_form, probs_b, d_mixed, preferred_element_type=jnp.float32
    ).astype(jnp.bfloat16)
    centre = jnp.sum(probs * d_probs, axis=-1, keepdims=True)
    d_scores = (probs * (d_probs - centre) * factor).astype(jnp.bfloat16)
    d_queries = jnp.einsum(
        "bhlm," + key_form + "->" + layout, d_scores, key_part, preferred_element_type=jnp.float32
    ).astype(jnp.bfloat16)
    d_keys = jnp.einsum(
        "bhlm," + layout + "->" + key_form, d_scores, queries, preferred_element_type=jnp.float32
    ).astype(jnp.bfloat16)
    joined = jnp.concatenate(
        [merge_heads(d_queries), merge_heads(d_keys), merge_heads(d_values)], axis=-1
    )
    d_normed = jnp.dot(joined, w_in.T, preferred_element_type=jnp.float32)
    scaled = d_normed * gain_vec
    d_tokens = inv_rms * (
        scaled - widened * inv_rms * inv_rms * jnp.mean(scaled * widened, axis=-1, keepdims=True)
    )
    return (upstream.astype(jnp.float32) + d_tokens).astype(jnp.bfloat16)


def line_forward(lines, gain_vec, w_in, w_out):
    feature_count = lines.shape[3]
    flat = lines.reshape(-1, lines.shape[2], feature_count)
    return forward_out(flat, gain_vec, w_in, w_out, "blhe").reshape(lines.shape)


def line_backward(lines, upstream, gain_vec, w_in, w_out):
    feature_count = lines.shape[3]
    flat = lines.reshape(-1, lines.shape[2], feature_count)
    flat_up = upstream.reshape(flat.shape)
    return backward(flat, flat_up, gain_vec, w_in, w_out, "blhe").reshape(lines.shape)


def per_device(tokens, cotangent, gain_x, wqkv_x, wo_x, gain_z, wqkv_z, wo_z):
    full_in_x, full_out_x = (
        lax.all_gather(wqkv_x, "tr", axis=0, tiled=True),
        lax.all_gather(wo_x, "tr", axis=0, tiled=True),
    )
    full_in_z, full_out_z = (
        lax.all_gather(wqkv_z, "tr", axis=0, tiled=True),
        lax.all_gather(wo_z, "tr", axis=0, tiled=True),
    )
    width = tokens.shape[-1]
    lines = lax.all_to_all(tokens, "tr", split_axis=1, concat_axis=2, tiled=True)
    cot_lines = lax.all_to_all(cotangent, "tr", split_axis=1, concat_axis=2, tiled=True)
    cells = lines.shape[1] * lines.shape[2]
    flat = (lines.shape[0], cells, width)
    cot_columns = lax.all_to_all(
        cot_lines.reshape(flat), "gz", split_axis=1, concat_axis=0, tiled=True
    )
    mid_lines = line_forward(lines, gain_x, full_in_x, full_out_x)
    mid_columns = lax.all_to_all(
        mid_lines.reshape(flat), "gz", split_axis=1, concat_axis=0, tiled=True
    )
    grad_columns = backward(
        mid_columns, cot_columns, gain_z, full_in_z, full_out_z, "lbhe"
    )
    grad_lines = lax.all_to_all(grad_columns, "gz", split_axis=0, concat_axis=1, tiled=True)
    result_lines = line_backward(lines, grad_lines.reshape(lines.shape), gain_x, full_in_x, full_out_x)
    return lax.all_to_all(result_lines, "tr", split_axis=2, concat_axis=1, tiled=True)


F32, BF16 = jnp.float32, jnp.bfloat16


def nt(a, b):
    return lax.dot_general(a, b, (((1,), (1,)), ((), ())), preferred_element_type=F32)


def tn(a, b):
    return lax.dot_general(a, b, (((0,), (0,)), ((), ())), preferred_element_type=F32)


def nn(a, b):
    return jnp.dot(a, b, preferred_element_type=F32)


def rms(a):
    return lax.rsqrt(jnp.mean(a * a, axis=-1, keepdims=True) + 1e-06)


def project(a, rstd, gain, w, qkv, before=None):
    width = a.shape[1]
    normed = (a * rstd * gain).astype(BF16)
    for j in range(3):
        if before is not None:
            before(j)
        cols = slice(j * width, (j + 1) * width)
        qkv[:, cols] = nn(normed, w[:, cols]).astype(BF16)


def line_mask(block, line, inner):
    key = lax.broadcasted_iota(jnp.int32, (block, block), 0)
    query = lax.broadcasted_iota(jnp.int32, (block, block), 1)
    if inner:
        return key % line == query % line
    return key // line == query // line


def head_spans(width):
    size = width // H
    return [[pl.ds(n * width + h * size, size) for n in range(3)] for h in range(H)]


def softmax_rows(qkv, at, spans, mask, factor):
    qk = [nt(qkv[at, sp[1]], qkv[at, sp[0]]) for sp in spans]
    scores = [jnp.where(mask, x * factor, -1e30) for x in qk]
    tops = [jnp.max(x, axis=0, keepdims=True) for x in scores]
    grown = [jnp.exp(x - t) for x, t in zip(scores, tops)]
    sums = [1.0 / jnp.sum(x, axis=0, keepdims=True) for x in grown]
    return [x * t for x, t in zip(grown, sums)]


def attend_scores(qkv, probs, first, mask):
    rows = qkv.shape[0]
    width = qkv.shape[1] // 3
    block = mask.shape[0]
    factor = 1.0 / math.sqrt(width // H)
    for b in range(rows // block):
        ps = softmax_rows(qkv, pl.ds(b * block, block), head_spans(width), mask, factor)
        for h, p in enumerate(ps):
            probs[(first + b) * H + h] = p


def attend_forward(qkv, probs, first, mixed, mask):
    rows, width = mixed.shape
    block = mask.shape[0]
    factor = 1.0 / math.sqrt(width // H)
    spans = head_spans(width)
    for b in range(rows // block):
        at = pl.ds(b * block, block)
        ps = softmax_rows(qkv, at, spans, mask, factor)
        for h, p in enumerate(ps):
            probs[(first + b) * H + h] = p
        outs = [tn(p.astype(BF16), qkv[at, sp[2]]) for p, sp in zip(ps, spans)]
        for sp, o in zip(spans, outs):
            mixed[at, sp[0]] = o.astype(BF16)


def attend_backward(qkv, probs, first, d_mixed, joined):
    rows, width = d_mixed.shape
    block = probs.shape[1]
    factor = 1.0 / math.sqrt(width // H)
    spans = head_spans(width)
    for b in range(rows // block):
        at = pl.ds(b * block, block)
        dps = [nt(qkv[at, sp[2]], d_mixed[at, sp[0]]) for sp in spans]
        ps = [probs[(first + b) * H + h] for h in range(H)]
        dvs = [nn(p.astype(BF16), d_mixed[at, sp[0]]) for p, sp in zip(ps, spans)]
        centres = [jnp.sum(p * dp, axis=0, keepdims=True) for p, dp in zip(ps, dps)]
        dss = [(p * (dp - c) * factor).astype(BF16) for p, dp, c in zip(ps, dps, centres)]
        dks = [nn(ds, qkv[at, sp[0]]) for ds, sp in zip(dss, spans)]
        dqs = [tn(ds, qkv[at, sp[1]]) for ds, sp in zip(dss, spans)]
        for sp, dq, dk, dv in zip(spans, dqs, dks, dvs):
            joined[at, sp[0]] = dq.astype(BF16)
            joined[at, sp[1]] = dk.astype(BF16)
            joined[at, sp[2]] = dv.astype(BF16)


def norm_backward(a, c, rstd, gain, joined, w, dn, turned):
    width = a.shape[-1]
    part = width // 3
    for j in range(3):
        cols = slice(j * part, (j + 1) * part)
        dn[:, cols] = nn(joined[...], w[:, cols]) if turned else nt(joined[...], w[cols, :])
    scaled = dn[...] * gain
    mean = jnp.mean(scaled * a, axis=-1, keepdims=True)
    return (c + rstd * (scaled - a * (rstd * rstd) * mean)).astype(BF16)


def kernel(
    nt_, ng, line_x,
    tok, cot, gain_x, wx, ox, gain_z, wz, oz, out,
    tokr, cotz, mids, midr, grads, gradr, outs,
    fwx, fox, fwz, foz, wxt, oxt, qkvx, qkvz, probs, probz, mixed, dmix, joined, dn, ax, az, cz,
    tr_send, tr_recv, gz_send, gz_recv, w_send, w_recv, c_send, c_recv, entered, local,
):
    me, mine = lax.axis_index("tr"), lax.axis_index("gz")
    sib, across = me + 1 - 2 * (me % 2), (me + 2) % nt_
    gy, gp = mine % 2, (mine // 2) % 2
    ynbr, znbr = mine + 1 - 2 * gy, mine + 2 - 4 * gp
    slab, pairs, width = tok.shape[0], tok.shape[3], tok.shape[5]
    parts = tok.shape[2]
    half = ax.shape[0] // parts
    block = half // 2

    def tell(sem, t, g):
        pl.semaphore_signal(sem, inc=1, device_id=(t, g), device_id_type=pl.DeviceIdType.MESH)

    zrow, last = mine // 2, ng // 2 - 1

    def tell_lanes(sem):
        for d in range(1, nt_):
            tell(sem, (me + d) % nt_, mine)

    def tell_near(sem):
        tell(sem, me, ynbr)
        pl.when(zrow > 0)(lambda: tell(sem, me, mine - 2))
        pl.when(zrow < last)(lambda: tell(sem, me, mine + 2))

    near = 1 + (zrow + last) // (last + 1) + (2 * last - zrow) // (last + 1)

    barrier = pltpu.get_barrier_semaphore()
    tell_lanes(barrier)
    if NEAR:
        tell_near(barrier)
    else:
        for d in range(1, ng):
            tell(barrier, me, (mine + d) % ng)

    own_w = ((wx, wx, wx, ox), (wz, wz, wz, oz))
    full_w = ((fwx, fwx, fwx, fox), (fwz, fwz, fwz, foz))
    depth = wx.shape[0]
    quarter = depth // 4

    here = [
        pltpu.make_async_copy(tok.at[:, me], tokr.at[:, :, :, me], local.at[0]),
    ]
    for s in range(2):
        for k in (0, 3):
            to = full_w[s][k].at[pl.ds(pl.multiple_of(me * depth, 16), depth)]
            here.append(pltpu.make_async_copy(own_w[s][k], to, local.at[len(here)]))
    for copy in here:
        copy.start()

    if NEAR:
        pl.semaphore_wait(barrier, nt_ - 1 + near)
        tell_near(entered.at[0])
    else:
        pl.semaphore_wait(barrier, nt_ + ng - 2)
        tell_lanes(entered.at[3])

    def widen(step):
        if step < 3:
            if NEAR:
                pl.semaphore_wait(entered.at[step], near)
                if step < 2:
                    tell_near(entered.at[step + 1])
                else:
                    tell_lanes(entered.at[3])
        else:
            pl.semaphore_wait(entered.at[3], nt_ - 1)

    def remote(src, dst, send, recv, t, g):
        return pltpu.make_async_remote_copy(
            src_ref=src, dst_ref=dst, send_sem=send, recv_sem=recv,
            device_id=(t, g), device_id_type=pl.DeviceIdType.MESH,
        )

    def own(s, k, row, n):
        at = pl.ds(pl.multiple_of(row, 16), n)
        return own_w[s][k].at[at, pl.ds((k % 3) * width, width)]

    def spot(s, k, shard, row, n):
        at = pl.ds(pl.multiple_of(shard * depth + row, 16), n)
        return full_w[s][k].at[at, pl.ds((k % 3) * width, width)]

    def push(s, k, role, src, dst, t, g):
        return remote(src, dst, w_send.at[s, k, role], w_recv.at[s, k, role], t, g)

    odd = (gy + gp) % 2
    q_me, q_d = (2 * odd + gy) * quarter, (2 * odd + 1 - gy) * quarter
    q_y, q_z = (3 - 2 * odd - gy) * quarter, (2 - 2 * odd + gy) * quarter
    by_z = (0, 1)

    def direct_rows(s, k):
        if s == 0 or DIRECT[k] == 0:
            return q_me, quarter
        if DIRECT[k] == 1:
            return 2 * odd * quarter, 2 * quarter
        n = DIRECT[k] * quarter
        return gy * (depth - n), n

    def relay_rows(s, k, sent):
        if s == 0 or DIRECT[k] <= 1:
            return (q_me if sent else q_y), quarter
        n = DIRECT[k] * quarter
        return (gy if sent else 1 - gy) * n, depth - n

    def over_z(s, k):
        return s == 0 or DIRECT[k] <= 1

    def role0(s, k):
        row, n = direct_rows(s, k)
        return push(s, k, 0, own(s, k, row, n), spot(s, k, me, row, n), across, mine)

    def role1(s, k):
        return push(s, k, 1, own(s, k, 0, depth), spot(s, k, me, 0, depth), sib, mine)

    def role2(s, k):
        row, n = relay_rows(s, k, True)
        at = spot(s, k, across, row, n)
        return push(s, k, 2, at, at, me, ynbr)

    def role3(s, k):
        at = spot(s, k, across, q_me, quarter)
        return push(s, k, 3, at, at, me, znbr)

    def role4(s, k):
        if k in by_z:
            at = spot(s, k, across, q_y, quarter)
            return push(s, k, 4, at, at, me, znbr)
        at = spot(s, k, across, q_z, quarter)
        return push(s, k, 4, at, at, me, ynbr)

    def two_steps(s, k):
        return s == 0 or DIRECT[k] == 0

    def role5(s, k):
        at = spot(s, k, across, 0, depth)
        return push(s, k, 5, at, at, sib, mine)

    def arrived(s, k, role):
        if role == 0:
            at = spot(s, k, across, *direct_rows(s, k))
        elif role == 1:
            at = spot(s, k, sib, 0, depth)
        elif role == 2:
            at = spot(s, k, across, *relay_rows(s, k, False))
        elif role == 3:
            at = spot(s, k, across, q_z, quarter)
        elif role == 4:
            at = spot(s, k, across, q_d, quarter)
        else:
            at = spot(s, k, (sib + 2) % nt_, 0, depth)
        push(s, k, role, at, at, sib, mine).wait_recv()

    turns = (mine // (ng // 2), 1 - mine // (ng // 2))

    def tr_copy(n, d):
        t = (me + d) % nt_
        src, dst = tr_ends(n, t, me)
        return remote(src, dst, tr_send.at[n, d], tr_recv.at[n, d], t, mine)

    def tr_ends(n, to, source):
        if n == 0:
            return tok.at[:, to], tokr.at[:, :, :, source]
        h, j = (n - 1) // 2, turns[(n - 1) % 2]
        pair = pl.ds(2 * j, 2)
        return outs.at[h, :, pair, to], out.at[:, source, h, pair]

    def gz_ends(n, to, source):
        if n < 2:
            h = n
            return mids.at[h, :, to // 2, :, to % 2], midr.at[h, pl.ds(source * slab, slab)]
        h = n - 2
        return grads.at[h, pl.ds(to * slab, slab)], gradr.at[h, :, source // 2, :, source % 2]

    def gz_copy(n, d):
        g = (mine + d) % ng
        src, dst = gz_ends(n, g, mine)
        return remote(src, dst, gz_send.at[n, d], gz_recv.at[n, d], me, g)

    far_first = [2, 3, 1] if nt_ == 4 else list(range(1, nt_))
    gz_order = sorted(range(1, ng), key=lambda d: -min(d, ng - d))

    def tr_begin(n):
        for d in far_first:
            tr_copy(n, d).start()

    def tr_end(n):
        for d in range(1, nt_):
            tr_copy(n, d).wait_send()
            src = (me + nt_ - d) % nt_
            at = tr_ends(n, me, src)[1]
            remote(at, at, tr_send.at[n, d], tr_recv.at[n, d], src, mine).wait_recv()

    def gz_begin(n):
        for d in gz_order:
            gz_copy(n, d).start()

    def gz_end(n):
        for d in range(1, ng):
            gz_copy(n, d).wait_send()
            src = (mine + ng - d) % ng
            at = gz_ends(n, mine, src)[1]
            remote(at, at, gz_send.at[n, d], gz_recv.at[n, d], me, src).wait_recv()

    core, zc, zs = me % 2, mine // 2, ng // 2
    lanes = (me, sib, across, (sib + 2) % nt_)

    def halves(j):
        return (0,) if j < 2 else range(parts)

    def cot_ends(j, to, z, source, at_x, h):
        if j < 2:
            return cot.at[:, to, :, z], cotz.at[pl.ds(source * slab, slab), :, at_x]
        return cot.at[:, to, h, z], cotz.at[pl.ds(source * slab, slab), h, at_x]

    def cot_copy(j, dz, h):
        z = (zc + dz) % zs
        src, dst = cot_ends(j, lanes[j], z, mine, me // 2, h)
        return remote(src, dst, c_send.at[j, dz, h], c_recv.at[j, dz, gy, h], lanes[j], 2 * z + core)

    def unless_self(j, dz, act):
        if j == 0 and dz == 0:
            pl.when(core != gy)(act)
        else:
            act()

    def cot_begin(js, h=0):
        for dz in (2, 1, 3, 0):
            for j in js:
                unless_self(j, dz, lambda: cot_copy(j, dz, h).start())

    def cot_end(h):
        other = (core + gy) % 2
        for i in range(2):
            if i == 0 and h > 0:
                continue
            at_x = (me // 2 + i) % 2
            for dz in range(zs):
                for ys in range(2):
                    g = 2 * ((zc + zs - dz) % zs) + ys
                    at = cot_ends(2 * i, me, zc, g, at_x, h)[1]
                    copy = remote(at, at, c_send.at[0, 0, 0], c_recv.at[other + 2 * i, dz, ys, h], sib, mine)
                    if i == 0 and dz == 0:
                        pl.when((core != gy) | (gy != ys))(lambda: copy.wait_recv())
                    else:
                        copy.wait_recv()
        if h == 0:
            pl.when(core == gy)(lambda: cot_self().wait())

    def cot_sent():
        for dz in range(zs):
            for j in range(4):
                for h in halves(j):
                    unless_self(j, dz, lambda: cot_copy(j, dz, h).wait_send())

    def cot_self():
        return pltpu.make_async_copy(cot.at[:, me, :, zc], cotz.at[pl.ds(mine * slab, slab), :, me // 2], local.at[7])

    ks = range(4)

    def begin_w1(pieces):
        for k in pieces:
            role0(1, k).start()

    for k in ks:
        role0(0, k).start()
    for k in ks:
        role1(0, k).start()
    pl.when(core == gy)(lambda: cot_self().start())
    for step in range(3):
        widen(step)
    if COT0 == 0:
        cot_begin((0,))
    if WIDE == 0:
        widen(3)
        cot_begin((1,))
    for k in ks:
        arrived(0, k, 0)
        role2(0, k).start()
        role3(0, k).start()
        if k == 0 and WIDE == 1:
            widen(3)
            if COT0 == 0:
                cot_begin((1,))
        if k == TOK_AFTER:
            tr_begin(0)
        begin_w1([j for j in ks if W1_AT[j] == k])
        if COT1 == k:
            cot_begin((2, 3))
    for k in ks:
        arrived(0, k, 2)
        if k in by_z:
            role4(0, k).start()
        arrived(0, k, 3)
        if k not in by_z:
            role4(0, k).start()
    if COT0 == 4:
        cot_begin((0, 1))
    begin_w1([j for j in ks if W1_AT[j] == 4])
    if COT1 == 4:
        cot_begin((2, 3))
        if COT2 < 0:
            cot_begin((2, 3), 1)
    for k in ks:
        arrived(0, k, 4)
        role5(0, k).start()
    for copy in here:
        copy.wait()
    tr_end(0)
    begin_w1([j for j in ks if W1_AT[j] == 5])
    if COT1 == 5:
        cot_begin((2, 3))
    for k in ks:
        role1(1, k).start()
    for h in range(parts):
        for j in range(2):
            ax[pl.ds(h * half + j * block, block)] = tokr[:, h, 2 * j : 2 * j + 2].reshape(block, width)
    for k in ks:
        arrived(0, k, 1)
        arrived(0, k, 5)

    def relay_z(pieces):
        for k in pieces:
            arrived(1, k, 0)
            role2(1, k).start()
            if over_z(1, k):
                role3(1, k).start()

    mask_x = line_mask(block, line_x, False)
    mask_z = line_mask(block, block // (slab * ng), True)
    gx, gz = gain_x[...][None], gain_z[...][None]
    for h in range(parts):
        at = pl.ds(h * half, half)
        a = ax[at].astype(F32)
        project(a, rms(a), gx, fwx, qkvx.at[at])
        attend_forward(qkvx.at[at], probs, 2 * h, mixed.at[at], mask_x)
        mid = ax[at].astype(F32) + nn(mixed[at], fox[...])
        mid = mid.astype(BF16)
        for j in range(2):
            spots = mids.at[h, :, 2 * j : 2 * j + 2]
            spots[...] = mid[j * block : (j + 1) * block].reshape(spots.shape)
        gz_begin(h)
        midr[h, pl.ds(mine * slab, slab)] = mids[h, :, mine // 2, :, mine % 2]
        if h == COT2:
            cot_begin((2, 3), 1)
        if h == 0:
            relay_z(RELAY1)
    def turn(pieces):
        for k in pieces:
            at = pl.ds((k % 3) * width, width)
            turned = (oxt if k == 3 else wxt).at[at]
            turned[...] = full_w[0][k][:, (k % 3) * width : (k % 3 + 1) * width].T

    turn(T0)
    relay_z([k for k in ks if k not in RELAY1])
    turn(T1)
    for k in ks:
        arrived(1, k, 2)
        if over_z(1, k):
            arrived(1, k, 3)
        if two_steps(1, k):
            role4(1, k).start()
        else:
            role5(1, k).start()
    for k in ks:
        if two_steps(1, k):
            arrived(1, k, 4)
            role5(1, k).start()

    def whole_z(k):
        arrived(1, k, 1)
        arrived(1, k, 5)


    def z_front(h):
        at = pl.ds(h * half, half)
        gz_end(h)
        for j in range(2):
            az[pl.ds(h * half + j * block, block)] = midr[h, :, j].reshape(block, width)
        a = az[at].astype(F32)
        rstd = rms(a)
        project(a, rstd, gz, fwz, qkvz.at[at], whole_z if h == 0 else None)
        attend_scores(qkvz.at[at], probz, 2 * h, mask_z)
        return rstd

    for h in range(parts):
        at = pl.ds(h * half, half)
        rstd = z_front(h)
        if h == 0:
            whole_z(3)
        cot_end(h)
        for j in range(2):
            cz[pl.ds(h * half + j * block, block)] = cotz[:, h, j].reshape(block, width)
        dmix[at] = nt(cz[at], foz[...]).astype(BF16)
        attend_backward(qkvz.at[at], probz, 2 * h, dmix.at[at], joined.at[at])
        back = norm_backward(
            az[at].astype(F32), cz[at].astype(F32), rstd, gz, joined.at[at], fwz, dn.at[at], False
        )
        for j in range(2):
            grads[h, :, j] = back[j * block : (j + 1) * block].reshape(slab * ng, block // (slab * ng), width)
        gz_begin(2 + h)
        gradr[h, :, mine // 2, :, mine % 2] = grads[h, pl.ds(mine * slab, slab)]

    def grads_here(n, j, near):
        count = ng // 2
        for d in range(1 if near else 0, count):
            g = j * count + ((mine + d) % count if near else d)
            at = gz_ends(n, mine, g)[1]
            remote(at, at, gz_send.at[n, 0], gz_recv.at[n, (mine + ng - g) % ng], me, g).wait_recv()

    turn(T2)
    kept = []
    for h in range(parts):
        for i, j in enumerate(turns):
            at = pl.ds(pl.multiple_of(h * half + j * block, 16), block)
            pair = pl.ds(2 * j, 2)
            a = ax[at].astype(F32)
            rstd = rms(a)
            grads_here(2 + h, j, i == 0)
            c = gradr[h, :, pair].reshape(block, width)
            dmix[at] = nn(c, oxt[...]).astype(BF16)
            attend_backward(qkvx.at[at], probs, 2 * h + j, dmix.at[at], joined.at[at])
            back = norm_backward(
                ax[at].astype(F32), c.astype(F32), rstd, gx, joined.at[at], wxt, dn.at[at], True
            )
            spots = outs.at[h, :, pair]
            spots[...] = back.reshape(spots.shape)
            n = 1 + 2 * h + i
            tr_begin(n)
            keep = pltpu.make_async_copy(*tr_ends(n, me, me), local.at[7 + n])
            keep.start()
            kept.append(keep)

    for k in ks:
        for s in range(2):
            role0(s, k).wait_send()
            role1(s, k).wait_send()
            role2(s, k).wait_send()
            role5(s, k).wait_send()
            if over_z(s, k):
                role3(s, k).wait_send()
            if two_steps(s, k):
                role4(s, k).wait_send()
    cot_sent()
    for h in range(parts):
        for d in range(1, ng):
            gz_copy(2 + h, d).wait_send()
    for n, keep in enumerate(kept):
        tr_end(1 + n)
        keep.wait()


DIRECT = (1, 1, 1, 1)
TOK_AFTER = 0
W1_AT = (3, 3, 3, 3)
COT0, COT1 = 0, 5
NEAR, WIDE = False, 0
RELAY1 = (0, 1, 2, 3)
COT2 = 1
T0, T1 = (0, 1), (2, 3)
T2 = ()
VM = 56


def settle(given, out, held, came, went):
    count = given.shape[0]
    ins = [pltpu.make_async_copy(given.at[i], held.at[i], came.at[i]) for i in range(count)]
    outs = [pltpu.make_async_copy(held.at[i], out.at[i], went.at[i]) for i in range(count)]
    for copy in ins:
        copy.start()
    for a, b in zip(ins, outs):
        a.wait()
        b.start()
    for copy in outs:
        copy.wait()


def fits_kernel(trs, gzs, slab, y, x_own, width, depth):
    return (trs, gzs, y, x_own) == (4, 8, 32, 2) and (slab * trs * x_own * 4) % 32 == 0 and width % 128 == 0 and depth % 64 == 0


def fused(trs, gzs, tokens, cotangent, gain_x, wqkv_x, wo_x, gain_z, wqkv_z, wo_z):
    slab, y, x_own, width = tokens.shape
    x, z = x_own * trs, slab * gzs
    rows = slab * y * x_own
    parts, group = 2, gzs // 2
    split = (slab, trs, parts, group, x_own, width)
    block = rows // 4
    lines = (slab, group, 2, trs // 2, x_own, width)
    vm = pl.BlockSpec(memory_space=pltpu.VMEM)
    hbm = pl.BlockSpec(memory_space=pl.ANY)
    wide = wqkv_x.shape[1]
    result = pl.pallas_call(
        functools.partial(kernel, trs, gzs, x),
        out_shape=jax.ShapeDtypeStruct(split, BF16),
        in_specs=[hbm, hbm, vm, hbm, hbm, vm, hbm, hbm],
        out_specs=hbm,
        scratch_shapes=[
            pltpu.VMEM((slab, parts, group, trs, x_own, width), BF16),
            pltpu.VMEM((z, parts, 2, x_own, width), BF16),
            pltpu.VMEM((parts, *lines), BF16),
            pltpu.VMEM((parts, z, 2, x_own, width), BF16),
            pltpu.VMEM((parts, z, 2, x_own, width), BF16),
            pltpu.VMEM((parts, *lines), BF16),
            pltpu.VMEM((parts, slab, group, trs, x_own, width), BF16),
        ]
        + [pltpu.VMEM((width, wide), BF16), pltpu.VMEM((width, width), BF16)] * 2
        + [pltpu.VMEM((wide, width), BF16), pltpu.VMEM((width, width), BF16)]
        + [pltpu.VMEM((rows, wide), BF16)] * 2
        + [pltpu.VMEM((4 * H, block, block), F32)] * 2
        + [pltpu.VMEM((rows, width), BF16)] * 2
        + [pltpu.VMEM((rows, wide), BF16), pltpu.VMEM((rows, width), F32)]
        + [pltpu.VMEM((rows, width), BF16)] * 3
        + [
            pltpu.SemaphoreType.DMA((5, trs)),
            pltpu.SemaphoreType.DMA((5, trs)),
            pltpu.SemaphoreType.DMA((4, gzs)),
            pltpu.SemaphoreType.DMA((4, gzs)),
            pltpu.SemaphoreType.DMA((2, 4, 6)),
            pltpu.SemaphoreType.DMA((2, 4, 6)),
            pltpu.SemaphoreType.DMA((4, gzs // 2, 2)),
            pltpu.SemaphoreType.DMA((4, gzs // 2, 2, 2)),
            pltpu.SemaphoreType.REGULAR((4,)),
            pltpu.SemaphoreType.DMA((12,)),
        ],
        compiler_params=pltpu.CompilerParams(
            collective_id=0, has_side_effects=True, vmem_limit_bytes=VM * 1024 * 1024
        ),
    )(
        tokens.reshape(split), cotangent.reshape(split),
        gain_x, wqkv_x, wo_x, gain_z, wqkv_z, wo_z,
    )
    return pl.pallas_call(
        settle,
        out_shape=jax.ShapeDtypeStruct(tokens.shape, BF16),
        in_specs=[hbm],
        out_specs=hbm,
        scratch_shapes=[
            pltpu.VMEM(tokens.shape, BF16),
            pltpu.SemaphoreType.DMA((slab,)),
            pltpu.SemaphoreType.DMA((slab,)),
        ],
    )(result.reshape(tokens.shape))


def solution(mesh):
    trs, gzs = mesh.shape["tr"], mesh.shape["gz"]

    def body(tokens, *rest):
        if fits_kernel(trs, gzs, *tokens.shape, rest[2].shape[0]):
            return fused(trs, gzs, tokens, *rest)
        return per_device(tokens, *rest)

    return jax.shard_map(
        body,
        mesh=mesh,
        in_specs=(
            P("gz", None, "tr", None),
            P("gz", None, "tr", None),
            P(),
            P("tr", None),
            P("tr", None),
            P(),
            P("tr", None),
            P("tr", None),
        ),
        out_specs=P("gz", None, "tr", None),
        check_vma=False,
    )
```
